128 devices in a mesh: ctx: 16 (over y, z), chan: 8 (over x, core).
Axes of the slice: x: 4, y: 4, z: 4, core: 2. Of those that a mesh axis runs over, the one named last changes fastest.
Arguments:
- signal: bfloat16 [8, 524288], P(None, ('ctx', 'chan')), may hold values from -0.015625 to 0.015625
- grad_out: bfloat16 [8, 524288], P(None, ('ctx', 'chan')), may hold values from -6 to 6
- residue: float32 [8, 16], P('chan'), may hold values from -2 to 2
- decay_rate: float32 [8, 16], P('chan'), may hold values from 1.9073486e-06 to 0.06
Outputs:
- grad_signal: bfloat16 [8, 524288], P(None, ('ctx', 'chan'))
- residue_grad: float32 [8, 16], P('chan')
- lograte_grad: float32 [8, 16], P('chan')
The draws below stay inside these ranges and needn't reach their ends.
All inputs are finite; a program needn't handle non-finite values.
Results may differ from the reference program's by a relative error of at most 0.013.
Values may be sent and summed in bfloat16 or wider, within the bound.
A program may use at most 192 MiB of HBM per device.

```python
import math
import jax
import jax.numpy as jnp
from jax import lax

LEN = 524288
ORDER = 16
CHANNELS = 8


def shard_levels(key, shape, pieces, smallest, high):
    def one(axis_at, blocks):
        steps = jax.random.uniform(jax.random.fold_in(jax.random.fold_in(key, 6), axis_at), (blocks,), jnp.float32, smallest / len(pieces), high / len(pieces))
        return jnp.repeat(jnp.exp(steps), shape[axis_at] // blocks).reshape((-1,) + (1,) * (len(shape) - axis_at - 1))

    loudness = one(*pieces[0])
    for cut in pieces[1:]:
        loudness = loudness * one(*cut)
    return loudness


def gaussian(key, shape, spread, most, cuts=(), kind=jnp.bfloat16):
    loudness = shard_levels(key, shape, cuts, -0.22, 0.18) if cuts else 1.0
    entries = jax.random.normal(key, shape, jnp.float32) * spread * loudness
    return jnp.minimum(jnp.maximum(entries, -most), most).astype(kind)


def setup_inputs(seed: int = 0) -> dict:
    key_of = jax.random.split(jax.random.key(seed), 5)
    return {
        "signal": gaussian(key_of[0], (CHANNELS, LEN), 0.003, 0.015625, ((1, 128),)),
        "grad_out": gaussian(key_of[1], (CHANNELS, LEN), 1.0, 6.0, ((1, 128),)),
        "residue": gaussian(key_of[2], (CHANNELS, ORDER), 0.35, 2.0, ((0, 8),), jnp.float32),
        "decay_rate": jnp.clip(jnp.exp(math.log(0.06) - 10.3563857 * jax.random.uniform(key_of[3], (CHANNELS, ORDER), jnp.float32) ** shard_levels(key_of[3], (CHANNELS, ORDER), ((0, 8),), -0.2, 0.2)), 1.9073486328125e-06, 0.06),
    }


def channel_grads(packed):
    row_signal, row_grad, row_residue, row_rate = packed
    positions = jnp.arange(LEN).astype(jnp.float32)
    decays = jnp.exp(-row_rate[:, None] * positions[None, :])
    root_rate = jnp.sqrt(row_rate)
    filter_row = jnp.dot(row_residue * root_rate, decays, precision=lax.Precision.HIGHEST)
    spec_signal = jnp.fft.rfft(row_signal.astype(jnp.float32), n=2 * LEN)
    spec_grad = jnp.fft.rfft(row_grad.astype(jnp.float32), n=2 * LEN)
    spec_filter = jnp.fft.rfft(filter_row, n=2 * LEN)
    grad_row = jnp.fft.irfft(jnp.conj(spec_filter) * spec_grad, n=2 * LEN)[:LEN]
    filter_grad = jnp.fft.irfft(spec_grad * jnp.conj(spec_signal), n=2 * LEN)[:LEN]
    residue_out = root_rate * jnp.dot(decays, filter_grad, precision=lax.Precision.HIGHEST)
    tilted = decays * (0.5 - row_rate[:, None] * positions[None, :])
    lograte_out = row_residue * root_rate * jnp.dot(tilted, filter_grad, precision=lax.Precision.HIGHEST)
    return (grad_row.astype(jnp.bfloat16), residue_out.astype(jnp.float32), lograte_out.astype(jnp.float32))

def reference(signal, grad_out, residue, decay_rate):
    return lax.map(channel_grads, (signal, grad_out, residue, decay_rate))
```

```python
import functools

import jax
import jax.numpy as jnp
from jax import lax
from jax.experimental import pallas as pl
from jax.experimental.pallas import tpu as pltpu
from jax.sharding import PartitionSpec as P

MESH = pl.DeviceIdType.MESH
LANES = 128
F32 = jnp.float32
BF16 = jnp.bfloat16


def split(value):
    high = value.astype(BF16)
    return high, (value - high.astype(F32)).astype(BF16)


def iota(shape, axis):
    return lax.broadcasted_iota(jnp.int32, shape, axis)


def lift(array, step):
    rows = array.shape[0]
    moved = pltpu.roll(array, rows - step, axis=0)
    return jnp.where(iota(array.shape, 0) < rows - step, moved, 0.0)


def scan(e, ed, rate, length):
    rows = e.shape[0]
    step = 1
    while step < rows:
        fade = jnp.exp(-rate * float(step * length))
        up, upd = lift(e, step), lift(ed, step)
        e, ed = e + fade * up, ed + fade * (upd + float(step * length) * up)
        step *= 2
    return e, ed


def combine(e, ed, x, xd, rate, length):
    rows = e.shape[0]
    incl, incld = scan(e, ed, rate, length)
    h, hd = lift(incl, 1), lift(incld, 1)
    back = ((rows - 1 - iota(x.shape, 0)) * length).astype(F32)
    fade = jnp.exp(-rate * back)
    x_all = jnp.sum(fade * x, axis=0, keepdims=True)
    xd_all = jnp.sum(fade * (xd + back * x), axis=0, keepdims=True)
    p = jnp.sum(x * h, axis=0, keepdims=True)
    pd = jnp.sum(xd * h + x * hd, axis=0, keepdims=True)
    return h, incl[0:1], incld[0:1], x_all, xd_all, p, pd


def pick(array, row):
    return jnp.sum(jnp.where(iota(array.shape, 0) == row, array, 0.0), axis=0, keepdims=True)


def tile(*rows):
    return jnp.concatenate(rows + (jnp.zeros((8 - len(rows), LANES), F32),), axis=0)


def kernel(
    ctx_n, chan_n,
    x_ref, g_ref, res_ref, rate_ref, y_ref, dres_ref, drate_ref,
    rows_x, rows_g, rows_y, corr_ref, par, mid, top,
    par_send, par_recv, mid_send, mid_recv, top_send, top_recv,
):
    ctx, chan = lax.axis_index("ctx"), lax.axis_index("chan")
    channels, span = x_ref.shape
    modes = res_ref.shape[1]
    chunks = span // LANES

    barrier = pltpu.get_barrier_semaphore()
    for r in range(1, chan_n):
        pl.semaphore_signal(
            barrier, inc=1, device_id={"chan": lax.rem(chan + r, chan_n)}, device_id_type=MESH
        )
    for r in range(1, ctx_n):
        pl.semaphore_signal(
            barrier, inc=1, device_id={"ctx": lax.rem(ctx + r, ctx_n)}, device_id_type=MESH
        )

    def exchange(buf, axis, me, n, send, recv):
        copies = []
        for r in range(1, n):
            copies.append(
                pltpu.make_async_remote_copy(
                    src_ref=buf.at[me],
                    dst_ref=buf.at[me],
                    send_sem=send.at[r],
                    recv_sem=recv.at[r],
                    device_id={axis: lax.rem(me + r, n)},
                    device_id_type=MESH,
                )
            )
        for copy in copies:
            copy.start()
        return copies

    repeats = LANES // modes
    par[chan] = tile(
        jnp.concatenate([res_ref[...]] * repeats, axis=1),
        jnp.concatenate([rate_ref[...]] * repeats, axis=1),
    )

    for n in range(chunks):
        rows_x[n * channels : (n + 1) * channels, :] = x_ref[:, n * LANES : (n + 1) * LANES].astype(F32)
        rows_g[n * channels : (n + 1) * channels, :] = g_ref[:, n * LANES : (n + 1) * LANES].astype(F32)
    xs = [rows_x[pl.ds(c, chunks, stride=channels), :].astype(BF16) for c in range(channels)]
    gs = [rows_g[pl.ds(c, chunks, stride=channels), :].astype(BF16) for c in range(channels)]
    down, across = iota((LANES, LANES), 0), iota((LANES, LANES), 1)
    lane8 = iota((8, LANES), 1)
    for c in range(channels):
        gram = lax.dot_general(xs[c], gs[c], (((0,), (0,)), ((), ())), preferred_element_type=F32)
        lags = gram[:8]
        for b in range(8, LANES, 8):
            moved = pltpu.roll(gram[b : b + 8], LANES - b, axis=1)
            lags += jnp.where(lane8 < LANES - b, moved, 0.0)
        corr_ref[c * 8 : (c + 1) * 8, :] = lags
    corr = corr_ref[pl.ds(0, channels, stride=8), :]
    for i in range(1, 8):
        moved = pltpu.roll(corr_ref[pl.ds(i, channels, stride=8), :], LANES - i, axis=1)
        corr += jnp.where(lane8 < LANES - i, moved, 0.0)

    pl.semaphore_wait(barrier, chan_n - 1 + ctx_n - 1)
    par_copies = exchange(par, "chan", chan, chan_n, par_send, par_recv)
    for copy in par_copies:
        copy.wait_recv()

    res8, rate8 = par[:, 0, :], par[:, 1, :]
    own = iota((chan_n, LANES), 1) // modes == iota((chan_n, LANES), 0)
    res = jnp.sum(jnp.where(own, res8, 0.0), axis=0, keepdims=True)
    rate = jnp.sum(jnp.where(own, rate8, 0.0), axis=0, keepdims=True)
    root = jnp.sqrt(rate)
    amp = res * root

    at = down.astype(F32)
    till = (LANES - down).astype(F32)
    decay_g, decay_x = jnp.exp(-rate * at), jnp.exp(-rate * till)

    def table(plain, weight):
        parts = split(plain), split(weight * plain)
        return jnp.concatenate(
            [jnp.concatenate([p[i] for p in parts], axis=1) for i in range(2)], axis=0
        )

    def twice(value):
        return jnp.concatenate([value, value], axis=1)

    corr_high, corr_low = split(corr)
    left_g = twice(jnp.concatenate(gs + [corr_high, corr_low], axis=0))
    left_x = twice(jnp.concatenate(xs, axis=0))
    raw_g = jnp.dot(left_g, table(decay_g, at), preferred_element_type=F32)
    raw_x = jnp.dot(left_x, table(decay_x, till), preferred_element_type=F32)
    lane_chan = iota((chunks, LANES), 1) // modes

    def by_channel(raw):
        plain = jnp.zeros((chunks, LANES), F32)
        weighted = plain
        for c in range(channels):
            part = raw[c * chunks : (c + 1) * chunks]
            plain = jnp.where(lane_chan == c, part[:, :LANES], plain)
            weighted = jnp.where(lane_chan == c, part[:, LANES:], weighted)
        return plain, weighted

    e, ed = by_channel(raw_g)
    x, xd = by_channel(raw_x)
    corr_rows = raw_g[channels * chunks :]
    corr_rows = corr_rows[:channels] + corr_rows[channels:]
    p_in = jnp.sum(jnp.where(own, corr_rows[:, :LANES], 0.0), axis=0, keepdims=True)
    pd_in = jnp.sum(jnp.where(own, corr_rows[:, LANES:], 0.0), axis=0, keepdims=True)

    h, e1, ed1, x1, xd1, p1, pd1 = combine(e, ed, x, xd, rate, LANES)
    mid[chan] = tile(e1, ed1, x1, xd1, p1 + p_in, pd1 + pd_in)
    mid_copies = exchange(mid, "chan", chan, chan_n, mid_send, mid_recv)

    lag = jnp.where(across[:channels] == 0, 0, LANES - across[:channels]).astype(F32)
    amp8 = res8 * jnp.sqrt(rate8)
    samples = jnp.zeros((channels, LANES), F32)
    for k in range(modes):
        samples += amp8[:, k : k + 1] * jnp.exp(-rate8[:, k : k + 1] * lag)
    for c in range(channels):
        spread = jnp.broadcast_to(samples[c : c + 1, :], (LANES, LANES))
        toeplitz = pltpu.roll(spread, 0, axis=1, stride=1, stride_axis=0)
        toeplitz = jnp.where(across <= down, toeplitz, 0.0)
        inner = jnp.dot(
            twice(gs[c]), jnp.concatenate(split(toeplitz), axis=0), preferred_element_type=F32
        )
        rows_y[c * chunks : (c + 1) * chunks, :] = inner

    for copy in mid_copies:
        copy.wait_recv()
    h2, e2, ed2, x2, xd2, p2, pd2 = combine(
        mid[:, 0, :], mid[:, 1, :], mid[:, 2, :], mid[:, 3, :], rate, span
    )
    p2 += jnp.sum(mid[:, 4, :], axis=0, keepdims=True)
    pd2 += jnp.sum(mid[:, 5, :], axis=0, keepdims=True)
    top[ctx] = tile(e2, ed2, x2, xd2, p2, pd2)
    top_copies = exchange(top, "ctx", ctx, ctx_n, top_send, top_recv)

    enter = pick(h2, chan)
    to_group_end = ((chan_n - 1 - chan) * span).astype(F32)
    group_fade = jnp.exp(-rate * to_group_end)
    to_end = ((chunks - 1 - iota((chunks, LANES), 0)) * LANES).astype(F32)
    chunk_fade = jnp.exp(-rate * to_end)
    out_high, out_low = split(amp * decay_x)
    out_table = jnp.concatenate(
        [twice(out_high), jnp.concatenate([out_low, jnp.zeros_like(out_low)], axis=1)], axis=0
    )

    for copy in top_copies:
        copy.wait_recv()
    h3, e3, ed3, x3, xd3, p3, pd3 = combine(
        top[:, 0, :], top[:, 1, :], top[:, 2, :], top[:, 3, :], rate, chan_n * span
    )
    enter = enter + group_fade * pick(h3, ctx)
    h = h + chunk_fade * enter
    lefts = []
    for c in range(channels):
        lefts.append(jnp.concatenate(split(jnp.where(lane_chan == c, h, 0.0)), axis=1))
    outer = lax.dot_general(
        jnp.concatenate(lefts, axis=0),
        out_table,
        (((1,), (1,)), ((), ())),
        preferred_element_type=F32,
    )
    total = rows_y[...] + outer[:, :LANES] + outer[:, LANES:]
    for c in range(channels):
        rows_g[pl.ds(c, chunks, stride=channels), :] = total[c * chunks : (c + 1) * chunks]
    for n in range(chunks):
        y_ref[:, n * LANES : (n + 1) * LANES] = rows_g[n * channels : (n + 1) * channels, :].astype(
            BF16
        )

    p3 += jnp.sum(top[:, 4, :], axis=0, keepdims=True)
    pd3 += jnp.sum(top[:, 5, :], axis=0, keepdims=True)
    final = tile(root * p3, amp * (0.5 * p3 - rate * pd3))
    final = pltpu.roll(final, lax.rem(LANES - modes * chan, LANES), axis=1)
    dres_ref[...] = final[0:1, :modes]
    drate_ref[...] = final[1:2, :modes]

    for copy in par_copies + mid_copies + top_copies:
        copy.wait_send()


def solution(mesh):
    ctx_n, chan_n = mesh.shape["ctx"], mesh.shape["chan"]

    def on_device(signal, grad_out, residue, decay_rate):
        channels, span = signal.shape
        modes = residue.shape[1]
        count = channels * span // LANES
        vmem = pl.BlockSpec(memory_space=pltpu.VMEM)
        small = jax.ShapeDtypeStruct((1, modes), F32)
        return pl.pallas_call(
            functools.partial(kernel, ctx_n, chan_n),
            out_shape=(jax.ShapeDtypeStruct((channels, span), BF16), small, small),
            in_specs=[vmem] * 4,
            out_specs=(vmem,) * 3,
            scratch_shapes=[
                pltpu.VMEM((count, LANES), F32),
                pltpu.VMEM((count, LANES), F32),
                pltpu.VMEM((count, LANES), F32),
                pltpu.VMEM((channels * 8, LANES), F32),
                pltpu.VMEM((chan_n, 8, LANES), F32),
                pltpu.VMEM((chan_n, 8, LANES), F32),
                pltpu.VMEM((ctx_n, 8, LANES), F32),
                pltpu.SemaphoreType.DMA((chan_n,)),
                pltpu.SemaphoreType.DMA((chan_n,)),
                pltpu.SemaphoreType.DMA((chan_n,)),
                pltpu.SemaphoreType.DMA((chan_n,)),
                pltpu.SemaphoreType.DMA((ctx_n,)),
                pltpu.SemaphoreType.DMA((ctx_n,)),
            ],
            compiler_params=pltpu.CompilerParams(
                collective_id=0, has_side_effects=True, vmem_limit_bytes=32 * 2**20
            ),
        )(signal, grad_out, residue, decay_rate)

    return jax.shard_map(
        on_device,
        mesh=mesh,
        in_specs=(
            P(None, ("ctx", "chan")),
            P(None, ("ctx", "chan")),
            P("chan", None),
            P("chan", None),
        ),
        out_specs=(P(None, ("ctx", "chan")), P("chan", None), P("chan", None)),
        check_vma=False,
    )
```

```python
import functools

import jax
import jax.numpy as jnp
from jax import lax
from jax.experimental import pallas as pl
from jax.experimental.pallas import tpu as pltpu
from jax.sharding import PartitionSpec as P

MESH = pl.DeviceIdType.MESH
LANES = 128
F32 = jnp.float32
BF16 = jnp.bfloat16


def split(value):
    high = value.astype(BF16)
    return high, (value - high.astype(F32)).astype(BF16)


def iota(shape, axis):
    return lax.broadcasted_iota(jnp.int32, shape, axis)


def lift(array, step):
    rows = array.shape[0]
    moved = pltpu.roll(array, rows - step, axis=0)
    return jnp.where(iota(array.shape, 0) < rows - step, moved, 0.0)


def scan(e, ed, rate, length):
    rows = e.shape[0]
    step = 1
    while step < rows:
        fade = jnp.exp(-rate * float(step * length))
        up, upd = lift(e, step), lift(ed, step)
        e, ed = e + fade * up, ed + fade * (upd + float(step * length) * up)
        step *= 2
    return e, ed


def combine(e, ed, x, xd, rate, length):
    rows = e.shape[0]
    incl, incld = scan(e, ed, rate, length)
    h, hd = lift(incl, 1), lift(incld, 1)
    back = ((rows - 1 - iota(x.shape, 0)) * length).astype(F32)
    fade = jnp.exp(-rate * back)
    x_all = jnp.sum(fade * x, axis=0, keepdims=True)
    xd_all = jnp.sum(fade * (xd + back * x), axis=0, keepdims=True)
    p = jnp.sum(x * h, axis=0, keepdims=True)
    pd = jnp.sum(xd * h + x * hd, axis=0, keepdims=True)
    return h, incl[0:1], incld[0:1], x_all, xd_all, p, pd


def kernel(
    ctx_n, chan_n,
    x_hbm, g_hbm, res_hbm, rate_hbm, y_ref, dres_ref, drate_ref,
    rows_x, rows_g, rows_y, corr_ref, par, out_stats, stats,
    x_ref, g_ref, res_ref, rate_ref, load_sem,
    par_send, par_recv, stats_send, stats_recv,
):
    ctx, chan = lax.axis_index("ctx"), lax.axis_index("chan")
    channels, span = x_ref.shape
    modes = res_ref.shape[1]
    chunks = span // LANES

    loads = [
        pltpu.make_async_copy(source, target, load_sem.at[i])
        for i, (source, target) in enumerate(
            [(res_hbm, res_ref), (rate_hbm, rate_ref), (x_hbm, x_ref), (g_hbm, g_ref)]
        )
    ]
    for load in loads:
        load.start()
    barrier = pltpu.get_barrier_semaphore()
    for r in range(1, chan_n):
        pl.semaphore_signal(
            barrier, inc=1, device_id={"chan": lax.rem(chan + r, chan_n)}, device_id_type=MESH
        )
    for r in range(1, ctx_n):
        pl.semaphore_signal(
            barrier, inc=1, device_id={"ctx": lax.rem(ctx + r, ctx_n)}, device_id_type=MESH
        )

    def exchange(buf, axis, me, n, send, recv):
        copies = []
        for r in range(1, n):
            copies.append(
                pltpu.make_async_remote_copy(
                    src_ref=buf.at[me],
                    dst_ref=buf.at[me],
                    send_sem=send.at[r],
                    recv_sem=recv.at[r],
                    device_id={axis: lax.rem(me + r, n)},
                    device_id_type=MESH,
                )
            )
        for copy in copies:
            copy.start()
        return copies

    loads[0].wait()
    loads[1].wait()
    repeats = LANES // modes
    par[chan, 0:1, :] = jnp.concatenate([res_ref[...]] * repeats, axis=1)
    par[chan, 1:2, :] = jnp.concatenate([rate_ref[...]] * repeats, axis=1)

    loads[2].wait()
    loads[3].wait()
    for n in range(chunks):
        rows_x[n * channels : (n + 1) * channels, :] = x_ref[:, n * LANES : (n + 1) * LANES].astype(F32)
        rows_g[n * channels : (n + 1) * channels, :] = g_ref[:, n * LANES : (n + 1) * LANES].astype(F32)
    xs = [rows_x[pl.ds(c, chunks, stride=channels), :].astype(BF16) for c in range(channels)]
    gs = [rows_g[pl.ds(c, chunks, stride=channels), :].astype(BF16) for c in range(channels)]
    down, across = iota((LANES, LANES), 0), iota((LANES, LANES), 1)
    lane8 = iota((8, LANES), 1)
    for c in range(channels):
        gram = lax.dot_general(xs[c], gs[c], (((0,), (0,)), ((), ())), preferred_element_type=F32)
        lags = gram[:8]
        for b in range(8, LANES, 8):
            moved = pltpu.roll(gram[b : b + 8], LANES - b, axis=1)
            lags += jnp.where(lane8 < LANES - b, moved, 0.0)
        corr_ref[c * 8 : (c + 1) * 8, :] = lags
    corr = corr_ref[pl.ds(0, channels, stride=8), :]
    for i in range(1, 8):
        moved = pltpu.roll(corr_ref[pl.ds(i, channels, stride=8), :], LANES - i, axis=1)
        corr += jnp.where(lane8 < LANES - i, moved, 0.0)

    pl.semaphore_wait(barrier, chan_n - 1 + ctx_n - 1)
    par_copies = exchange(par, "chan", chan, chan_n, par_send, par_recv)
    for copy in par_copies:
        copy.wait_recv()

    res8, rate8 = par[:, 0, :], par[:, 1, :]
    own = iota((chan_n, LANES), 1) // modes == iota((chan_n, LANES), 0)
    res = jnp.sum(jnp.where(own, res8, 0.0), axis=0, keepdims=True)
    rate = jnp.sum(jnp.where(own, rate8, 0.0), axis=0, keepdims=True)
    root = jnp.sqrt(rate)
    amp = res * root

    at = down.astype(F32)
    till = (LANES - down).astype(F32)
    decay_g, decay_x = jnp.exp(-rate * at), jnp.exp(-rate * till)

    def table(plain, weight):
        parts = split(plain), split(weight * plain)
        return jnp.concatenate(
            [jnp.concatenate([p[i] for p in parts], axis=1) for i in range(2)], axis=0
        )

    def twice(value):
        return jnp.concatenate([value, value], axis=1)

    corr_high, corr_low = split(corr)
    left_g = twice(jnp.concatenate(gs + [corr_high, corr_low], axis=0))
    left_x = twice(jnp.concatenate(xs, axis=0))
    raw_g = jnp.dot(left_g, table(decay_g, at), preferred_element_type=F32)
    raw_x = jnp.dot(left_x, table(decay_x, till), preferred_element_type=F32)
    lane_chan = iota((chunks, LANES), 1) // modes

    def by_channel(raw):
        plain = jnp.zeros((chunks, LANES), F32)
        weighted = plain
        for c in range(channels):
            part = raw[c * chunks : (c + 1) * chunks]
            plain = jnp.where(lane_chan == c, part[:, :LANES], plain)
            weighted = jnp.where(lane_chan == c, part[:, LANES:], weighted)
        return plain, weighted

    e, ed = by_channel(raw_g)
    x, xd = by_channel(raw_x)
    corr_rows = raw_g[channels * chunks :]
    corr_rows = corr_rows[:channels] + corr_rows[channels:]
    p_in = jnp.sum(jnp.where(own, corr_rows[:, :LANES], 0.0), axis=0, keepdims=True)
    pd_in = jnp.sum(jnp.where(own, corr_rows[:, LANES:], 0.0), axis=0, keepdims=True)

    h, e1, ed1, x1, xd1, p1, pd1 = combine(e, ed, x, xd, rate, LANES)
    sums = [e1, ed1, x1, xd1, p1 + p_in, pd1 + pd_in]
    owner_row = iota((chan_n, LANES), 0)
    lane_group = iota((chan_n, LANES), 1) // modes
    for_owner = jnp.zeros((chan_n, LANES), F32)
    for q, value in enumerate(sums):
        moved = pltpu.roll(value, modes * q, axis=1) if q else value
        for_owner = jnp.where(lane_group == (owner_row + q) % chan_n, moved, for_owner)
    out_stats[:, 0, :] = jnp.broadcast_to(e1, (chan_n, LANES))
    out_stats[:, 1, :] = for_owner
    count = ctx_n * chan_n
    me = ctx * chan_n + chan

    @pl.loop(0, count - 1)
    def _(i):
        to = i + jnp.where(i >= me, 1, 0)
        to_chan = lax.rem(to, chan_n)
        pltpu.make_async_remote_copy(
            src_ref=out_stats.at[to_chan],
            dst_ref=stats.at[me],
            send_sem=stats_send,
            recv_sem=stats_recv,
            device_id={"ctx": lax.div(to, chan_n), "chan": to_chan},
            device_id_type=MESH,
        ).start()

    stats[me] = out_stats[chan]

    lag = jnp.where(across[:channels] == 0, 0, LANES - across[:channels]).astype(F32)
    amp8 = res8 * jnp.sqrt(rate8)
    samples = jnp.zeros((channels, LANES), F32)
    for k in range(modes):
        samples += amp8[:, k : k + 1] * jnp.exp(-rate8[:, k : k + 1] * lag)
    for c in range(channels):
        spread = jnp.broadcast_to(samples[c : c + 1, :], (LANES, LANES))
        toeplitz = pltpu.roll(spread, 0, axis=1, stride=1, stride_axis=0)
        toeplitz = jnp.where(across <= down, toeplitz, 0.0)
        inner = jnp.dot(
            twice(gs[c]), jnp.concatenate(split(toeplitz), axis=0), preferred_element_type=F32
        )
        rows_y[c * chunks : (c + 1) * chunks, :] = inner

    to_end = ((chunks - 1 - iota((chunks, LANES), 0)) * LANES).astype(F32)
    chunk_fade = jnp.exp(-rate * to_end)
    out_high, out_low = split(amp * decay_x)
    out_table = jnp.concatenate(
        [twice(out_high), jnp.concatenate([out_low, jnp.zeros_like(out_low)], axis=1)], axis=0
    )
    ahead = iota((count, LANES), 0) - (me + 1)
    fade_in = jnp.exp(-rate * (jnp.maximum(ahead, 0) * span).astype(F32))
    fade_in = jnp.where(ahead >= 0, fade_in, 0.0)

    everyone = stats.at[pl.ds(0, count - 1)]
    pltpu.make_async_copy(everyone, everyone, stats_recv).wait()
    enter = jnp.sum(fade_in * stats[:, 0, :], axis=0, keepdims=True)
    h = h + chunk_fade * enter
    lefts = []
    for c in range(channels):
        lefts.append(jnp.concatenate(split(jnp.where(lane_chan == c, h, 0.0)), axis=1))
    outer = lax.dot_general(
        jnp.concatenate(lefts, axis=0),
        out_table,
        (((1,), (1,)), ((), ())),
        preferred_element_type=F32,
    )
    total = rows_y[...] + outer[:, :LANES] + outer[:, LANES:]
    for c in range(channels):
        rows_g[pl.ds(c, chunks, stride=channels), :] = total[c * chunks : (c + 1) * chunks]
    for n in range(chunks):
        y_ref[:, n * LANES : (n + 1) * LANES] = rows_g[n * channels : (n + 1) * channels, :].astype(
            BF16
        )

    mine = stats[:, 1, :]
    groups = [
        pltpu.roll(mine, lax.rem(2 * LANES - modes * (chan + q), LANES), axis=1) for q in range(6)
    ]
    own_res, own_rate = par[chan, 0:1, :], par[chan, 1:2, :]
    *_, plain, tilted = combine(*groups[:4], own_rate, span)
    plain += jnp.sum(groups[4], axis=0, keepdims=True)
    tilted += jnp.sum(groups[5], axis=0, keepdims=True)
    own_root = jnp.sqrt(own_rate)
    dres_ref[...] = (own_root * plain)[:, :modes]
    drate_ref[...] = (own_res * own_root * (0.5 * plain - own_rate * tilted))[:, :modes]

    pltpu.make_async_copy(everyone, everyone, stats_send).wait()
    for copy in par_copies:
        copy.wait_send()


def solution(mesh):
    ctx_n, chan_n = mesh.shape["ctx"], mesh.shape["chan"]

    def on_device(signal, grad_out, residue, decay_rate):
        channels, span = signal.shape
        modes = residue.shape[1]
        count = channels * span // LANES
        vmem = pl.BlockSpec(memory_space=pltpu.VMEM)
        small = jax.ShapeDtypeStruct((1, modes), F32)
        return pl.pallas_call(
            functools.partial(kernel, ctx_n, chan_n),
            out_shape=(jax.ShapeDtypeStruct((channels, span), BF16), small, small),
            in_specs=[pl.BlockSpec(memory_space=pl.ANY)] * 4,
            out_specs=(vmem,) * 3,
            scratch_shapes=[
                pltpu.VMEM((count, LANES), F32),
                pltpu.VMEM((count, LANES), F32),
                pltpu.VMEM((count, LANES), F32),
                pltpu.VMEM((channels * 8, LANES), F32),
                pltpu.VMEM((chan_n, 2, LANES), F32),
                pltpu.VMEM((chan_n, 2, LANES), F32),
                pltpu.VMEM((ctx_n * chan_n, 2, LANES), F32),
                pltpu.VMEM((channels, span), BF16),
                pltpu.VMEM((channels, span), BF16),
                pltpu.VMEM((1, modes), F32),
                pltpu.VMEM((1, modes), F32),
                pltpu.SemaphoreType.DMA((4,)),
                pltpu.SemaphoreType.DMA((chan_n,)),
                pltpu.SemaphoreType.DMA((chan_n,)),
                pltpu.SemaphoreType.DMA,
                pltpu.SemaphoreType.DMA,
            ],
            compiler_params=pltpu.CompilerParams(
                collective_id=0, has_side_effects=True, vmem_limit_bytes=60 * 2**20
            ),
        )(signal, grad_out, residue, decay_rate)

    return jax.shard_map(
        on_device,
        mesh=mesh,
        in_specs=(
            P(None, ("ctx", "chan")),
            P(None, ("ctx", "chan")),
            P("chan", None),
            P("chan", None),
        ),
        out_specs=(P(None, ("ctx", "chan")), P("chan", None), P("chan", None)),
        check_vma=False,
    )
```

```python
import functools

import jax
import jax.numpy as jnp
from jax import lax
from jax.experimental import pallas as pl
from jax.experimental.pallas import tpu as pltpu
from jax.sharding import PartitionSpec as P

MESH = pl.DeviceIdType.MESH
LANES = 128
F32 = jnp.float32
BF16 = jnp.bfloat16


def split(value):
    high = value.astype(BF16)
    return high, (value - high.astype(F32)).astype(BF16)


def iota(shape, axis):
    return lax.broadcasted_iota(jnp.int32, shape, axis)


def lift(array, step):
    rows = array.shape[0]
    moved = pltpu.roll(array, rows - step, axis=0)
    return jnp.where(iota(array.shape, 0) < rows - step, moved, 0.0)


def scan(e, ed, rate, length):
    rows = e.shape[0]
    step = 1
    while step < rows:
        fade = jnp.exp(-rate * float(step * length))
        up, upd = lift(e, step), lift(ed, step)
        e, ed = e + fade * up, ed + fade * (upd + float(step * length) * up)
        step *= 2
    return e, ed


def combine(e, ed, x, xd, rate, length):
    rows = e.shape[0]
    incl, incld = scan(e, ed, rate, length)
    h, hd = lift(incl, 1), lift(incld, 1)
    back = ((rows - 1 - iota(x.shape, 0)) * length).astype(F32)
    fade = jnp.exp(-rate * back)
    x_all = jnp.sum(fade * x, axis=0, keepdims=True)
    xd_all = jnp.sum(fade * (xd + back * x), axis=0, keepdims=True)
    p = jnp.sum(x * h, axis=0, keepdims=True)
    pd = jnp.sum(xd * h + x * hd, axis=0, keepdims=True)
    return h, incl[0:1], incld[0:1], x_all, xd_all, p, pd


def kernel(
    ctx_n, chan_n,
    x_hbm, g_hbm, res_hbm, rate_hbm, y_ref, small_ref,
    rows_x, rows_g, rows_y, corr_ref, par, out_stats, stats,
    x_ref, g_ref, res_ref, rate_ref, load_sem,
    par_send, par_recv, stats_send, stats_recv,
):
    ctx, chan = lax.axis_index("ctx"), lax.axis_index("chan")
    channels, span = x_ref.shape
    modes = res_ref.shape[1]
    chunks = span // LANES

    loads = [
        pltpu.make_async_copy(source, target, load_sem.at[i])
        for i, (source, target) in enumerate(
            [(res_hbm, res_ref), (rate_hbm, rate_ref), (x_hbm, x_ref), (g_hbm, g_ref)]
        )
    ]
    for load in loads:
        load.start()
    barrier = pltpu.get_barrier_semaphore()
    for r in range(1, chan_n):
        pl.semaphore_signal(
            barrier, inc=1, device_id={"chan": lax.rem(chan + r, chan_n)}, device_id_type=MESH
        )
    for r in range(1, ctx_n):
        pl.semaphore_signal(
            barrier, inc=1, device_id={"ctx": lax.rem(ctx + r, ctx_n)}, device_id_type=MESH
        )

    def exchange(buf, axis, me, n, send, recv):
        copies = []
        for r in range(1, n):
            copies.append(
                pltpu.make_async_remote_copy(
                    src_ref=buf.at[me],
                    dst_ref=buf.at[me],
                    send_sem=send.at[r],
                    recv_sem=recv.at[r],
                    device_id={axis: lax.rem(me + r, n)},
                    device_id_type=MESH,
                )
            )
        for copy in copies:
            copy.start()
        return copies

    loads[0].wait()
    loads[1].wait()
    repeats = LANES // modes
    par[chan, 0:1, :] = jnp.concatenate([res_ref[...]] * repeats, axis=1)
    par[chan, 1:2, :] = jnp.concatenate([rate_ref[...]] * repeats, axis=1)

    loads[2].wait()
    loads[3].wait()
    for n in range(chunks):
        rows_x[n * channels : (n + 1) * channels, :] = x_ref[:, n * LANES : (n + 1) * LANES].astype(F32)
        rows_g[n * channels : (n + 1) * channels, :] = g_ref[:, n * LANES : (n + 1) * LANES].astype(F32)
    xs = [rows_x[pl.ds(c, chunks, stride=channels), :].astype(BF16) for c in range(channels)]
    gs = [rows_g[pl.ds(c, chunks, stride=channels), :].astype(BF16) for c in range(channels)]
    down, across = iota((LANES, LANES), 0), iota((LANES, LANES), 1)
    lane8 = iota((8, LANES), 1)
    for c in range(channels):
        gram = lax.dot_general(xs[c], gs[c], (((0,), (0,)), ((), ())), preferred_element_type=F32)
        lags = gram[:8]
        for b in range(8, LANES, 8):
            moved = pltpu.roll(gram[b : b + 8], LANES - b, axis=1)
            lags += jnp.where(lane8 < LANES - b, moved, 0.0)
        corr_ref[c * 8 : (c + 1) * 8, :] = lags
    corr = corr_ref[pl.ds(0, channels, stride=8), :]
    for i in range(1, 8):
        moved = pltpu.roll(corr_ref[pl.ds(i, channels, stride=8), :], LANES - i, axis=1)
        corr += jnp.where(lane8 < LANES - i, moved, 0.0)

    pl.semaphore_wait(barrier, chan_n - 1 + ctx_n - 1)
    par_copies = exchange(par, "chan", chan, chan_n, par_send, par_recv)
    for copy in par_copies:
        copy.wait_recv()

    res8, rate8 = par[:, 0, :], par[:, 1, :]
    own = iota((chan_n, LANES), 1) // modes == iota((chan_n, LANES), 0)
    res = jnp.sum(jnp.where(own, res8, 0.0), axis=0, keepdims=True)
    rate = jnp.sum(jnp.where(own, rate8, 0.0), axis=0, keepdims=True)
    root = jnp.sqrt(rate)
    amp = res * root

    at = down.astype(F32)
    till = (LANES - down).astype(F32)
    decay_g, decay_x = jnp.exp(-rate * at), jnp.exp(-rate * till)

    def table(plain, weight):
        parts = split(plain), split(weight * plain)
        return jnp.concatenate(
            [jnp.concatenate([p[i] for p in parts], axis=1) for i in range(2)], axis=0
        )

    def twice(value):
        return jnp.concatenate([value, value], axis=1)

    corr_high, corr_low = split(corr)
    left_g = twice(jnp.concatenate(gs + [corr_high, corr_low], axis=0))
    left_x = twice(jnp.concatenate(xs, axis=0))
    raw_g = jnp.dot(left_g, table(decay_g, at), preferred_element_type=F32)
    raw_x = jnp.dot(left_x, table(decay_x, till), preferred_element_type=F32)
    lane_chan = iota((chunks, LANES), 1) // modes

    def by_channel(raw):
        plain = jnp.zeros((chunks, LANES), F32)
        weighted = plain
        for c in range(channels):
            part = raw[c * chunks : (c + 1) * chunks]
            plain = jnp.where(lane_chan == c, part[:, :LANES], plain)
            weighted = jnp.where(lane_chan == c, part[:, LANES:], weighted)
        return plain, weighted

    e, ed = by_channel(raw_g)
    x, xd = by_channel(raw_x)
    corr_rows = raw_g[channels * chunks :]
    corr_rows = corr_rows[:channels] + corr_rows[channels:]
    p_in = jnp.sum(jnp.where(own, corr_rows[:, :LANES], 0.0), axis=0, keepdims=True)
    pd_in = jnp.sum(jnp.where(own, corr_rows[:, LANES:], 0.0), axis=0, keepdims=True)

    h, e1, ed1, x1, xd1, p1, pd1 = combine(e, ed, x, xd, rate, LANES)
    sums = [e1, ed1, x1, xd1, p1 + p_in, pd1 + pd_in]
    owner_row = iota((chan_n, LANES), 0)
    lane_group = iota((chan_n, LANES), 1) // modes
    for_owner = jnp.zeros((chan_n, LANES), F32)
    for q, value in enumerate(sums):
        moved = pltpu.roll(value, modes * q, axis=1) if q else value
        for_owner = jnp.where(lane_group == (owner_row + q) % chan_n, moved, for_owner)
    out_stats[:, 0, :] = jnp.broadcast_to(e1, (chan_n, LANES))
    out_stats[:, 1, :] = for_owner
    count = ctx_n * chan_n
    me = ctx * chan_n + chan

    @pl.loop(0, count - 1)
    def _(i):
        to = i + jnp.where(i >= me, 1, 0)
        to_chan = lax.rem(to, chan_n)
        pltpu.make_async_remote_copy(
            src_ref=out_stats.at[to_chan],
            dst_ref=stats.at[me],
            send_sem=stats_send,
            recv_sem=stats_recv,
            device_id={"ctx": lax.div(to, chan_n), "chan": to_chan},
            device_id_type=MESH,
        ).start()

    stats[me] = out_stats[chan]

    lag = jnp.where(across[:channels] == 0, 0, LANES - across[:channels]).astype(F32)
    amp8 = res8 * jnp.sqrt(rate8)
    samples = jnp.zeros((channels, LANES), F32)
    for k in range(modes):
        samples += amp8[:, k : k + 1] * jnp.exp(-rate8[:, k : k + 1] * lag)
    for c in range(channels):
        spread = jnp.broadcast_to(samples[c : c + 1, :], (LANES, LANES))
        toeplitz = pltpu.roll(spread, 0, axis=1, stride=1, stride_axis=0)
        toeplitz = jnp.where(across <= down, toeplitz, 0.0)
        inner = jnp.dot(
            twice(gs[c]), jnp.concatenate(split(toeplitz), axis=0), preferred_element_type=F32
        )
        rows_y[c * chunks : (c + 1) * chunks, :] = inner

    to_end = ((chunks - 1 - iota((chunks, LANES), 0)) * LANES).astype(F32)
    chunk_fade = jnp.exp(-rate * to_end)
    out_high, out_low = split(amp * decay_x)
    out_table = jnp.concatenate(
        [twice(out_high), jnp.concatenate([out_low, jnp.zeros_like(out_low)], axis=1)], axis=0
    )
    ahead = iota((count, LANES), 0) - (me + 1)
    fade_in = jnp.exp(-rate * (jnp.maximum(ahead, 0) * span).astype(F32))
    fade_in = jnp.where(ahead >= 0, fade_in, 0.0)

    everyone = stats.at[pl.ds(0, count - 1)]
    pltpu.make_async_copy(everyone, everyone, stats_recv).wait()
    enter = jnp.sum(fade_in * stats[:, 0, :], axis=0, keepdims=True)
    h = h + chunk_fade * enter
    lefts = []
    for c in range(channels):
        lefts.append(jnp.concatenate(split(jnp.where(lane_chan == c, h, 0.0)), axis=1))
    outer = lax.dot_general(
        jnp.concatenate(lefts, axis=0),
        out_table,
        (((1,), (1,)), ((), ())),
        preferred_element_type=F32,
    )
    total = rows_y[...] + outer[:, :LANES] + outer[:, LANES:]
    for c in range(channels):
        rows_g[pl.ds(c, chunks, stride=channels), :] = total[c * chunks : (c + 1) * chunks]
    for n in range(chunks):
        y_ref[:, n * LANES : (n + 1) * LANES] = rows_g[n * channels : (n + 1) * channels, :].astype(
            BF16
        )

    mine = stats[:, 1, :]
    groups = [
        pltpu.roll(mine, lax.rem(2 * LANES - modes * (chan + q), LANES), axis=1) for q in range(6)
    ]
    own_res, own_rate = par[chan, 0:1, :], par[chan, 1:2, :]
    *_, plain, tilted = combine(*groups[:4], own_rate, span)
    plain += jnp.sum(groups[4], axis=0, keepdims=True)
    tilted += jnp.sum(groups[5], axis=0, keepdims=True)
    own_root = jnp.sqrt(own_rate)
    small_ref[0:1, :] = own_root * plain
    small_ref[1:2, :] = own_res * own_root * (0.5 * plain - own_rate * tilted)

    pltpu.make_async_copy(everyone, everyone, stats_send).wait()
    for copy in par_copies:
        copy.wait_send()


def solution(mesh):
    ctx_n, chan_n = mesh.shape["ctx"], mesh.shape["chan"]

    def on_device(signal, grad_out, residue, decay_rate):
        channels, span = signal.shape
        modes = residue.shape[1]
        count = channels * span // LANES
        pinned = [pltpu.with_memory_space_constraint(v, pltpu.HBM) for v in (signal, grad_out, residue, decay_rate)]
        vmem = pl.BlockSpec(memory_space=pltpu.VMEM)
        small = jax.ShapeDtypeStruct((2, LANES), F32)
        y, small = pl.pallas_call(
            functools.partial(kernel, ctx_n, chan_n),
            out_shape=(jax.ShapeDtypeStruct((channels, span), BF16), small),
            in_specs=[pl.BlockSpec(memory_space=pl.ANY)] * 4,
            out_specs=(vmem,) * 2,
            scratch_shapes=[
                pltpu.VMEM((count, LANES), F32),
                pltpu.VMEM((count, LANES), F32),
                pltpu.VMEM((count, LANES), F32),
                pltpu.VMEM((channels * 8, LANES), F32),
                pltpu.VMEM((chan_n, 2, LANES), F32),
                pltpu.VMEM((chan_n, 2, LANES), F32),
                pltpu.VMEM((ctx_n * chan_n, 2, LANES), F32),
                pltpu.VMEM((channels, span), BF16),
                pltpu.VMEM((channels, span), BF16),
                pltpu.VMEM((1, modes), F32),
                pltpu.VMEM((1, modes), F32),
                pltpu.SemaphoreType.DMA((4,)),
                pltpu.SemaphoreType.DMA((chan_n,)),
                pltpu.SemaphoreType.DMA((chan_n,)),
                pltpu.SemaphoreType.DMA,
                pltpu.SemaphoreType.DMA,
            ],
            compiler_params=pltpu.CompilerParams(
                collective_id=0, has_side_effects=True, vmem_limit_bytes=32 * 2**20
            ),
        )(*pinned)
        return y, small[0:1, :modes], small[1:2, :modes]

    return jax.shard_map(
        on_device,
        mesh=mesh,
        in_specs=(
            P(None, ("ctx", "chan")),
            P(None, ("ctx", "chan")),
            P("chan", None),
            P("chan", None),
        ),
        out_specs=(P(None, ("ctx", "chan")), P("chan", None), P("chan", None)),
        check_vma=False,
    )
```

```python
import functools

import jax
import jax.numpy as jnp
from jax import lax
from jax.experimental import pallas as pl
from jax.experimental.pallas import tpu as pltpu
from jax.sharding import PartitionSpec as P

MESH = pl.DeviceIdType.MESH
LANES = 128
F32 = jnp.float32
BF16 = jnp.bfloat16


def split(value):
    high = value.astype(BF16)
    return high, (value - high.astype(F32)).astype(BF16)


def iota(shape, axis):
    return lax.broadcasted_iota(jnp.int32, shape, axis)


def lift(array, step):
    rows = array.shape[0]
    moved = pltpu.roll(array, rows - step, axis=0)
    return jnp.where(iota(array.shape, 0) < rows - step, moved, 0.0)


def scan_fades(rate, rows, length):
    return [jnp.exp(-rate * float(length << i)) for i in range((rows - 1).bit_length())]


def entering(e, ed, fades, length):
    for i, fade in enumerate(fades):
        step = 1 << i
        up, upd = lift(e, step), lift(ed, step)
        e, ed = e + fade * up, ed + fade * (upd + float(step * length) * up)
    return lift(e, 1), lift(ed, 1), e[0:1], ed[0:1]


def total_over(rows):
    return jnp.sum(rows, axis=0, keepdims=True)


def kernel(
    ctx_n, chan_n,
    x_hbm, g_hbm, res_hbm, rate_hbm, y_ref, small_ref,
    rows_x, rows_g, rows_y, rows_f, corr_ref, par, out_stats, stats,
    x_ref, g_ref, res_ref, rate_ref, load_sem,
    par_send, par_recv, stats_send, stats_recv,
):
    ctx, chan = lax.axis_index("ctx"), lax.axis_index("chan")
    channels, span = x_ref.shape
    modes = res_ref.shape[1]
    chunks = span // LANES

    loads = [
        pltpu.make_async_copy(source, target, load_sem.at[i])
        for i, (source, target) in enumerate(
            [(res_hbm, res_ref), (rate_hbm, rate_ref), (x_hbm, x_ref), (g_hbm, g_ref)]
        )
    ]
    for load in loads:
        load.start()
    barrier = pltpu.get_barrier_semaphore()
    for r in range(1, chan_n):
        pl.semaphore_signal(
            barrier, inc=1, device_id={"chan": lax.rem(chan + r, chan_n)}, device_id_type=MESH
        )
    for r in range(1, ctx_n):
        pl.semaphore_signal(
            barrier, inc=1, device_id={"ctx": lax.rem(ctx + r, ctx_n)}, device_id_type=MESH
        )

    def exchange(buf, axis, me, n, send, recv):
        copies = []
        for r in range(1, n):
            copies.append(
                pltpu.make_async_remote_copy(
                    src_ref=buf.at[me],
                    dst_ref=buf.at[me],
                    send_sem=send.at[r],
                    recv_sem=recv.at[r],
                    device_id={axis: lax.rem(me + r, n)},
                    device_id_type=MESH,
                )
            )
        for copy in copies:
            copy.start()
        return copies

    loads[0].wait()
    loads[1].wait()
    repeats = LANES // modes
    par[chan, 0:1, :] = jnp.concatenate([res_ref[...]] * repeats, axis=1)
    par[chan, 1:2, :] = jnp.concatenate([rate_ref[...]] * repeats, axis=1)

    pl.semaphore_wait(barrier, chan_n - 1 + ctx_n - 1)
    par_copies = exchange(par, "chan", chan, chan_n, par_send, par_recv)

    loads[2].wait()
    loads[3].wait()
    for n in range(chunks):
        rows_x[n * channels : (n + 1) * channels, :] = x_ref[:, n * LANES : (n + 1) * LANES].astype(F32)
        rows_g[n * channels : (n + 1) * channels, :] = g_ref[:, n * LANES : (n + 1) * LANES].astype(F32)
    xs = [rows_x[pl.ds(c, chunks, stride=channels), :].astype(BF16) for c in range(channels)]
    gs = [rows_g[pl.ds(c, chunks, stride=channels), :].astype(BF16) for c in range(channels)]
    down, across = iota((LANES, LANES), 0), iota((LANES, LANES), 1)
    lane8 = iota((8, LANES), 1)
    for c in range(channels):
        gram = lax.dot_general(xs[c], gs[c], (((0,), (0,)), ((), ())), preferred_element_type=F32)
        lags = gram[:8]
        for b in range(8, LANES, 8):
            moved = pltpu.roll(gram[b : b + 8], LANES - b, axis=1)
            lags += jnp.where(lane8 < LANES - b, moved, 0.0)
        corr_ref[c * 8 : (c + 1) * 8, :] = lags
    corr = corr_ref[pl.ds(0, channels, stride=8), :]
    for i in range(1, 8):
        moved = pltpu.roll(corr_ref[pl.ds(i, channels, stride=8), :], LANES - i, axis=1)
        corr += jnp.where(lane8 < LANES - i, moved, 0.0)

    for copy in par_copies:
        copy.wait_recv()

    res8, rate8 = par[:, 0, :], par[:, 1, :]
    own = iota((chan_n, LANES), 1) // modes == iota((chan_n, LANES), 0)
    res = jnp.sum(jnp.where(own, res8, 0.0), axis=0, keepdims=True)
    rate = jnp.sum(jnp.where(own, rate8, 0.0), axis=0, keepdims=True)
    root = jnp.sqrt(rate)
    amp = res * root

    chunk_fades = scan_fades(rate, chunks, LANES)
    to_end = ((chunks - 1 - iota((chunks, LANES), 0)) * LANES).astype(F32)
    chunk_fade = jnp.exp(-rate * to_end)
    at = down.astype(F32)
    till = (LANES - down).astype(F32)
    decay_g, decay_x = jnp.exp(-rate * at), jnp.exp(-rate * till)

    def table(plain, weight):
        parts = split(plain), split(weight * plain)
        return jnp.concatenate(
            [jnp.concatenate([p[i] for p in parts], axis=1) for i in range(2)], axis=0
        )

    def twice(value):
        return jnp.concatenate([value, value], axis=1)

    corr_high, corr_low = split(corr)
    left_g = twice(jnp.concatenate(gs + [corr_high, corr_low], axis=0))
    left_x = twice(jnp.concatenate(xs, axis=0))
    raw_g = jnp.dot(left_g, table(decay_g, at), preferred_element_type=F32)
    raw_x = jnp.dot(left_x, table(decay_x, till), preferred_element_type=F32)
    lane_chan = iota((chunks, LANES), 1) // modes

    def by_channel(raw):
        plain = jnp.zeros((chunks, LANES), F32)
        weighted = plain
        for c in range(channels):
            part = raw[c * chunks : (c + 1) * chunks]
            plain = jnp.where(lane_chan == c, part[:, :LANES], plain)
            weighted = jnp.where(lane_chan == c, part[:, LANES:], weighted)
        return plain, weighted

    e, ed = by_channel(raw_g)
    x, xd = by_channel(raw_x)
    corr_rows = raw_g[channels * chunks :]
    corr_rows = corr_rows[:channels] + corr_rows[channels:]
    p_in = jnp.sum(jnp.where(own, corr_rows[:, :LANES], 0.0), axis=0, keepdims=True)
    pd_in = jnp.sum(jnp.where(own, corr_rows[:, LANES:], 0.0), axis=0, keepdims=True)

    h, hd, e1, ed1 = entering(e, ed, chunk_fades, LANES)
    x1 = total_over(chunk_fade * x)
    xd1 = total_over(chunk_fade * (xd + to_end * x))
    p1 = p_in + total_over(x * h)
    pd1 = pd_in + total_over(xd * h + x * hd)
    sums = [ed1, x1, xd1, p1, pd1]
    owner_row = iota((chan_n, LANES), 0)
    lane_group = iota((chan_n, LANES), 1) // modes
    for_owner = jnp.zeros((chan_n, LANES), F32)
    for q, value in enumerate(sums):
        moved = pltpu.roll(value, modes * q, axis=1) if q else value
        for_owner = jnp.where(lane_group == (owner_row + q) % chan_n, moved, for_owner)
    out_stats[:, 0, :] = jnp.broadcast_to(e1, (chan_n, LANES))
    out_stats[:, 1, :] = for_owner
    count = ctx_n * chan_n
    me = ctx * chan_n + chan

    @pl.loop(0, count - 1)
    def _(i):
        to = i + jnp.where(i >= me, 1, 0)
        to_chan = lax.rem(to, chan_n)
        pltpu.make_async_remote_copy(
            src_ref=out_stats.at[to_chan],
            dst_ref=stats.at[me],
            send_sem=stats_send,
            recv_sem=stats_recv,
            device_id={"ctx": lax.div(to, chan_n), "chan": to_chan},
            device_id_type=MESH,
        ).start()

    stats[me] = out_stats[chan]

    lag = jnp.where(across[:channels] == 0, 0, LANES - across[:channels]).astype(F32)
    amp8 = res8 * jnp.sqrt(rate8)
    samples = jnp.zeros((channels, LANES), F32)
    for k in range(modes):
        samples += amp8[:, k : k + 1] * jnp.exp(-rate8[:, k : k + 1] * lag)
    out_high, out_low = split(amp * decay_x)
    out_table = jnp.concatenate(
        [twice(out_high), jnp.concatenate([out_low, jnp.zeros_like(out_low)], axis=1)], axis=0
    )

    def expand(states):
        outer = lax.dot_general(
            jnp.concatenate(split(states), axis=1),
            out_table,
            (((1,), (1,)), ((), ())),
            preferred_element_type=F32,
        )
        return outer[:, :LANES] + outer[:, LANES:]

    local = expand(
        jnp.concatenate([jnp.where(lane_chan == c, h, 0.0) for c in range(channels)], axis=0)
    )
    for c in range(channels):
        spread = jnp.broadcast_to(samples[c : c + 1, :], (LANES, LANES))
        toeplitz = pltpu.roll(spread, 0, axis=1, stride=1, stride_axis=0)
        toeplitz = jnp.where(across <= down, toeplitz, 0.0)
        inner = jnp.dot(
            twice(gs[c]), jnp.concatenate(split(toeplitz), axis=0), preferred_element_type=F32
        )
        rows_y[pl.ds(c, chunks, stride=channels), :] = inner + local[c * chunks : (c + 1) * chunks]

    for n in range(chunks):
        rows_x[n * channels : (n + 1) * channels, :] = jnp.where(own, chunk_fade[n : n + 1], 0.0)
    ahead = iota((count, LANES), 0) - (me + 1)
    fade_in = jnp.exp(-rate * (jnp.maximum(ahead, 0) * span).astype(F32))
    rows_f[...] = jnp.where(ahead >= 0, fade_in, 0.0)
    span_fades = scan_fades(rate, count, span)

    everyone = stats.at[pl.ds(0, count - 1)]
    pltpu.make_async_copy(everyone, everyone, stats_recv).wait()
    states, mine = stats[:, 0, :], stats[:, 1, :]
    enter = total_over(rows_f[...] * states)
    y = rows_y[...] + expand(rows_x[...] * enter)
    for n in range(chunks):
        y_ref[:, n * LANES : (n + 1) * LANES] = y[n * channels : (n + 1) * channels].astype(BF16)

    def shifted(value, q):
        return pltpu.roll(value, LANES - modes * q, axis=1)

    h, hd, _, _ = entering(states, mine, span_fades, span)
    x, xd = shifted(mine, 1), shifted(mine, 2)
    sums = total_over(mine)
    plain = shifted(sums, 3) + total_over(x * h)
    tilted = shifted(sums, 4) + total_over(xd * h + x * hd)
    final = jnp.concatenate([root * plain, amp * (0.5 * plain - rate * tilted)], axis=0)
    small_ref[...] = pltpu.roll(final, lax.rem(LANES - modes * chan, LANES), axis=1)

    pltpu.make_async_copy(everyone, everyone, stats_send).wait()
    for copy in par_copies:
        copy.wait_send()


def solution(mesh):
    ctx_n, chan_n = mesh.shape["ctx"], mesh.shape["chan"]

    def on_device(signal, grad_out, residue, decay_rate):
        channels, span = signal.shape
        modes = residue.shape[1]
        count = channels * span // LANES
        pinned = [pltpu.with_memory_space_constraint(v, pltpu.HBM) for v in (signal, grad_out, residue, decay_rate)]
        vmem = pl.BlockSpec(memory_space=pltpu.VMEM)
        small = jax.ShapeDtypeStruct((2, LANES), F32)
        y, small = pl.pallas_call(
            functools.partial(kernel, ctx_n, chan_n),
            out_shape=(jax.ShapeDtypeStruct((channels, span), BF16), small),
            in_specs=[pl.BlockSpec(memory_space=pl.ANY)] * 4,
            out_specs=(vmem,) * 2,
            scratch_shapes=[
                pltpu.VMEM((count, LANES), F32),
                pltpu.VMEM((count, LANES), F32),
                pltpu.VMEM((count, LANES), F32),
                pltpu.VMEM((ctx_n * chan_n, LANES), F32),
                pltpu.VMEM((channels * 8, LANES), F32),
                pltpu.VMEM((chan_n, 2, LANES), F32),
                pltpu.VMEM((chan_n, 2, LANES), F32),
                pltpu.VMEM((ctx_n * chan_n, 2, LANES), F32),
                pltpu.VMEM((channels, span), BF16),
                pltpu.VMEM((channels, span), BF16),
                pltpu.VMEM((1, modes), F32),
                pltpu.VMEM((1, modes), F32),
                pltpu.SemaphoreType.DMA((4,)),
                pltpu.SemaphoreType.DMA((chan_n,)),
                pltpu.SemaphoreType.DMA((chan_n,)),
                pltpu.SemaphoreType.DMA,
                pltpu.SemaphoreType.DMA,
            ],
            compiler_params=pltpu.CompilerParams(
                collective_id=0, has_side_effects=True, vmem_limit_bytes=32 * 2**20
            ),
        )(*pinned)
        return y, small[0:1, :modes], small[1:2, :modes]

    return jax.shard_map(
        on_device,
        mesh=mesh,
        in_specs=(
            P(None, ("ctx", "chan")),
            P(None, ("ctx", "chan")),
            P("chan", None),
            P("chan", None),
        ),
        out_specs=(P(None, ("ctx", "chan")), P("chan", None), P("chan", None)),
        check_vma=False,
    )
```

```python
import functools

import jax
import jax.numpy as jnp
from jax import lax
from jax.experimental import pallas as pl
from jax.experimental.pallas import tpu as pltpu
from jax.sharding import PartitionSpec as P

MESH = pl.DeviceIdType.MESH
LANES = 128
F32 = jnp.float32
BF16 = jnp.bfloat16


def split(value):
    high = value.astype(BF16)
    return high, (value - high.astype(F32)).astype(BF16)


def iota(shape, axis):
    return lax.broadcasted_iota(jnp.int32, shape, axis)


def lift(array, step):
    rows = array.shape[0]
    moved = pltpu.roll(array, rows - step, axis=0)
    return jnp.where(iota(array.shape, 0) < rows - step, moved, 0.0)


def scan_fades(rate, rows, length):
    return [jnp.exp(-rate * float(length << i)) for i in range((rows - 1).bit_length())]


def entering(e, ed, fades, length):
    for i, fade in enumerate(fades):
        step = 1 << i
        up, upd = lift(e, step), lift(ed, step)
        e, ed = e + fade * up, ed + fade * (upd + float(step * length) * up)
    return lift(e, 1), lift(ed, 1), e[0:1], ed[0:1]


def farthest_first(n):
    return sorted(range(1, n), key=lambda r: -min(r, n - r))


def total_over(rows):
    return jnp.sum(rows, axis=0, keepdims=True)


def kernel(
    ctx_n, chan_n,
    x_hbm, g_hbm, res_hbm, rate_hbm, y_ref, small_ref,
    rows_x, rows_g, rows_y, rows_f, corr_ref, par, out_stats, stats,
    x_ref, g_ref, res_ref, rate_ref, load_sem,
    par_send, par_recv, stats_send, stats_recv,
):
    ctx, chan = lax.axis_index("ctx"), lax.axis_index("chan")
    channels, span = x_ref.shape
    modes = res_ref.shape[1]
    chunks = span // LANES

    loads = [
        pltpu.make_async_copy(source, target, load_sem.at[i])
        for i, (source, target) in enumerate(
            [(res_hbm, res_ref), (rate_hbm, rate_ref), (x_hbm, x_ref), (g_hbm, g_ref)]
        )
    ]
    loads[0].start()
    loads[1].start()
    barrier = pltpu.get_barrier_semaphore()
    for r in farthest_first(chan_n):
        pl.semaphore_signal(
            barrier, inc=1, device_id={"chan": lax.rem(chan + r, chan_n)}, device_id_type=MESH
        )
    for r in range(1, ctx_n):
        pl.semaphore_signal(
            barrier, inc=1, device_id={"ctx": lax.rem(ctx + r, ctx_n)}, device_id_type=MESH
        )
    loads[2].start()
    loads[3].start()

    def exchange(buf, axis, me, n, send, recv):
        copies = []
        for r in farthest_first(n):
            copies.append(
                pltpu.make_async_remote_copy(
                    src_ref=buf.at[me],
                    dst_ref=buf.at[me],
                    send_sem=send,
                    recv_sem=recv,
                    device_id={axis: lax.rem(me + r, n)},
                    device_id_type=MESH,
                )
            )
        for copy in copies:
            copy.start()

    loads[0].wait()
    loads[1].wait()
    repeats = LANES // modes
    par[chan, 0:1, :] = jnp.concatenate([res_ref[...]] * repeats, axis=1)
    par[chan, 1:2, :] = jnp.concatenate([rate_ref[...]] * repeats, axis=1)

    pl.semaphore_wait(barrier, chan_n - 1 + ctx_n - 1)
    exchange(par, "chan", chan, chan_n, par_send, par_recv)

    loads[2].wait()
    loads[3].wait()
    for n in range(chunks):
        rows_x[n * channels : (n + 1) * channels, :] = x_ref[:, n * LANES : (n + 1) * LANES].astype(F32)
        rows_g[n * channels : (n + 1) * channels, :] = g_ref[:, n * LANES : (n + 1) * LANES].astype(F32)
    xs = [rows_x[pl.ds(c, chunks, stride=channels), :].astype(BF16) for c in range(channels)]
    gs = [rows_g[pl.ds(c, chunks, stride=channels), :].astype(BF16) for c in range(channels)]
    down, across = iota((LANES, LANES), 0), iota((LANES, LANES), 1)
    lane8 = iota((8, LANES), 1)
    for c in range(channels):
        gram = lax.dot_general(xs[c], gs[c], (((0,), (0,)), ((), ())), preferred_element_type=F32)
        lags = gram[:8]
        for b in range(8, LANES, 8):
            moved = pltpu.roll(gram[b : b + 8], LANES - b, axis=1)
            lags += jnp.where(lane8 < LANES - b, moved, 0.0)
        corr_ref[c * 8 : (c + 1) * 8, :] = lags
    corr = corr_ref[pl.ds(0, channels, stride=8), :]
    for i in range(1, 8):
        moved = pltpu.roll(corr_ref[pl.ds(i, channels, stride=8), :], LANES - i, axis=1)
        corr += jnp.where(lane8 < LANES - i, moved, 0.0)

    others = par.at[pl.ds(0, chan_n - 1)]
    pltpu.make_async_copy(others, others, par_recv).wait()

    res8, rate8 = par[:, 0, :], par[:, 1, :]
    own = iota((chan_n, LANES), 1) // modes == iota((chan_n, LANES), 0)
    res = jnp.sum(jnp.where(own, res8, 0.0), axis=0, keepdims=True)
    rate = jnp.sum(jnp.where(own, rate8, 0.0), axis=0, keepdims=True)
    root = jnp.sqrt(rate)
    amp = res * root

    chunk_fades = scan_fades(rate, chunks, LANES)
    to_end = ((chunks - 1 - iota((chunks, LANES), 0)) * LANES).astype(F32)
    chunk_fade = jnp.exp(-rate * to_end)
    at = down.astype(F32)
    till = (LANES - down).astype(F32)
    decay_g, decay_x = jnp.exp(-rate * at), jnp.exp(-rate * till)

    def table(plain, weight):
        parts = split(plain), split(weight * plain)
        return jnp.concatenate(
            [jnp.concatenate([p[i] for p in parts], axis=1) for i in range(2)], axis=0
        )

    def twice(value):
        return jnp.concatenate([value, value], axis=1)

    corr_high, corr_low = split(corr)
    left_g = twice(jnp.concatenate(gs + [corr_high, corr_low], axis=0))
    left_x = twice(jnp.concatenate(xs, axis=0))
    raw_g = jnp.dot(left_g, table(decay_g, at), preferred_element_type=F32)
    raw_x = jnp.dot(left_x, table(decay_x, till), preferred_element_type=F32)
    lane_chan = iota((chunks, LANES), 1) // modes

    def by_channel(raw):
        plain = jnp.zeros((chunks, LANES), F32)
        weighted = plain
        for c in range(channels):
            part = raw[c * chunks : (c + 1) * chunks]
            plain = jnp.where(lane_chan == c, part[:, :LANES], plain)
            weighted = jnp.where(lane_chan == c, part[:, LANES:], weighted)
        return plain, weighted

    e, ed = by_channel(raw_g)
    x, xd = by_channel(raw_x)
    corr_rows = raw_g[channels * chunks :]
    corr_rows = corr_rows[:channels] + corr_rows[channels:]
    p_in = jnp.sum(jnp.where(own, corr_rows[:, :LANES], 0.0), axis=0, keepdims=True)
    pd_in = jnp.sum(jnp.where(own, corr_rows[:, LANES:], 0.0), axis=0, keepdims=True)

    h, hd, e1, ed1 = entering(e, ed, chunk_fades, LANES)
    x1 = total_over(chunk_fade * x)
    xd1 = total_over(chunk_fade * (xd + to_end * x))
    p1 = p_in + total_over(x * h)
    pd1 = pd_in + total_over(xd * h + x * hd)
    sums = [ed1, x1, xd1, p1, pd1]
    owner_row = iota((chan_n, LANES), 0)
    lane_group = iota((chan_n, LANES), 1) // modes
    for_owner = jnp.zeros((chan_n, LANES), F32)
    for q, value in enumerate(sums):
        moved = pltpu.roll(value, modes * q, axis=1) if q else value
        for_owner = jnp.where(lane_group == (owner_row + q) % chan_n, moved, for_owner)
    out_stats[:, 0, :] = jnp.broadcast_to(e1, (chan_n, LANES))
    out_stats[:, 1, :] = for_owner
    count = ctx_n * chan_n
    me = ctx * chan_n + chan

    @pl.loop(0, count - 1)
    def _(i):
        to = i + jnp.where(i >= me, 1, 0)
        to_chan = lax.rem(to, chan_n)
        pltpu.make_async_remote_copy(
            src_ref=out_stats.at[to_chan],
            dst_ref=stats.at[me],
            send_sem=stats_send,
            recv_sem=stats_recv,
            device_id={"ctx": lax.div(to, chan_n), "chan": to_chan},
            device_id_type=MESH,
        ).start()

    stats[me] = out_stats[chan]

    lag = jnp.where(across[:channels] == 0, 0, LANES - across[:channels]).astype(F32)
    amp8 = res8 * jnp.sqrt(rate8)
    samples = jnp.zeros((channels, LANES), F32)
    for k in range(modes):
        samples += amp8[:, k : k + 1] * jnp.exp(-rate8[:, k : k + 1] * lag)
    out_high, out_low = split(amp * decay_x)
    out_table = jnp.concatenate(
        [twice(out_high), jnp.concatenate([out_low, jnp.zeros_like(out_low)], axis=1)], axis=0
    )

    def expand(states):
        outer = lax.dot_general(
            jnp.concatenate(split(states), axis=1),
            out_table,
            (((1,), (1,)), ((), ())),
            preferred_element_type=F32,
        )
        return outer[:, :LANES] + outer[:, LANES:]

    local = expand(
        jnp.concatenate([jnp.where(lane_chan == c, h, 0.0) for c in range(channels)], axis=0)
    )
    for c in range(channels):
        spread = jnp.broadcast_to(samples[c : c + 1, :], (LANES, LANES))
        toeplitz = pltpu.roll(spread, 0, axis=1, stride=1, stride_axis=0)
        toeplitz = jnp.where(across <= down, toeplitz, 0.0)
        inner = jnp.dot(
            twice(gs[c]), jnp.concatenate(split(toeplitz), axis=0), preferred_element_type=F32
        )
        rows_y[pl.ds(c, chunks, stride=channels), :] = inner + local[c * chunks : (c + 1) * chunks]

    for n in range(chunks):
        rows_x[n * channels : (n + 1) * channels, :] = jnp.where(own, chunk_fade[n : n + 1], 0.0)
    ahead = iota((count, LANES), 0) - (me + 1)
    fade_in = jnp.exp(-rate * (jnp.maximum(ahead, 0) * span).astype(F32))
    rows_f[...] = jnp.where(ahead >= 0, fade_in, 0.0)
    span_fades = scan_fades(rate, count, span)

    everyone = stats.at[pl.ds(0, count - 1)]
    pltpu.make_async_copy(everyone, everyone, stats_send).wait()
    pltpu.make_async_copy(others, others, par_send).wait()
    pltpu.make_async_copy(everyone, everyone, stats_recv).wait()
    states, mine = stats[:, 0, :], stats[:, 1, :]
    enter = total_over(rows_f[...] * states)
    y = rows_y[...] + expand(rows_x[...] * enter)
    for n in range(chunks):
        y_ref[:, n * LANES : (n + 1) * LANES] = y[n * channels : (n + 1) * channels].astype(BF16)

    def shifted(value, q):
        return pltpu.roll(value, LANES - modes * q, axis=1)

    h, hd, _, _ = entering(states, mine, span_fades, span)
    x, xd = shifted(mine, 1), shifted(mine, 2)
    sums = total_over(mine)
    plain = shifted(sums, 3) + total_over(x * h)
    tilted = shifted(sums, 4) + total_over(xd * h + x * hd)
    final = jnp.concatenate([root * plain, amp * (0.5 * plain - rate * tilted)], axis=0)
    small_ref[...] = pltpu.roll(final, lax.rem(LANES - modes * chan, LANES), axis=1)


def solution(mesh):
    ctx_n, chan_n = mesh.shape["ctx"], mesh.shape["chan"]

    def on_device(signal, grad_out, residue, decay_rate):
        channels, span = signal.shape
        modes = residue.shape[1]
        count = channels * span // LANES
        pinned = [pltpu.with_memory_space_constraint(v, pltpu.HBM) for v in (signal, grad_out, residue, decay_rate)]
        vmem = pl.BlockSpec(memory_space=pltpu.VMEM)
        small = jax.ShapeDtypeStruct((2, LANES), F32)
        y, small = pl.pallas_call(
            functools.partial(kernel, ctx_n, chan_n),
            out_shape=(jax.ShapeDtypeStruct((channels, span), BF16), small),
            in_specs=[pl.BlockSpec(memory_space=pl.ANY)] * 4,
            out_specs=(vmem,) * 2,
            scratch_shapes=[
                pltpu.VMEM((count, LANES), F32),
                pltpu.VMEM((count, LANES), F32),
                pltpu.VMEM((count, LANES), F32),
                pltpu.VMEM((ctx_n * chan_n, LANES), F32),
                pltpu.VMEM((channels * 8, LANES), F32),
                pltpu.VMEM((chan_n, 2, LANES), F32),
                pltpu.VMEM((chan_n, 2, LANES), F32),
                pltpu.VMEM((ctx_n * chan_n, 2, LANES), F32),
                pltpu.VMEM((channels, span), BF16),
                pltpu.VMEM((channels, span), BF16),
                pltpu.VMEM((1, modes), F32),
                pltpu.VMEM((1, modes), F32),
                pltpu.SemaphoreType.DMA((4,)),
                pltpu.SemaphoreType.DMA,
                pltpu.SemaphoreType.DMA,
                pltpu.SemaphoreType.DMA,
                pltpu.SemaphoreType.DMA,
            ],
            compiler_params=pltpu.CompilerParams(
                collective_id=0, has_side_effects=True, vmem_limit_bytes=32 * 2**20
            ),
        )(*pinned)
        return y, small[0:1, :modes], small[1:2, :modes]

    return jax.shard_map(
        on_device,
        mesh=mesh,
        in_specs=(
            P(None, ("ctx", "chan")),
            P(None, ("ctx", "chan")),
            P("chan", None),
            P("chan", None),
        ),
        out_specs=(P(None, ("ctx", "chan")), P("chan", None), P("chan", None)),
        check_vma=False,
    )
```

```python
import functools

import jax
import jax.numpy as jnp
from jax import lax
from jax.experimental import pallas as pl
from jax.experimental.pallas import tpu as pltpu
from jax.sharding import PartitionSpec as P

MESH = pl.DeviceIdType.MESH
LANES = 128
F32 = jnp.float32
BF16 = jnp.bfloat16


def split(value):
    high = value.astype(BF16)
    return high, (value - high.astype(F32)).astype(BF16)


def iota(shape, axis):
    return lax.broadcasted_iota(jnp.int32, shape, axis)


def lift(array, step):
    rows = array.shape[0]
    moved = pltpu.roll(array, rows - step, axis=0)
    return jnp.where(iota(array.shape, 0) < rows - step, moved, 0.0)


def scan_fades(rate, rows, length):
    return [jnp.exp(-rate * float(length << i)) for i in range((rows - 1).bit_length())]


def entering(e, ed, fades, length):
    for i, fade in enumerate(fades):
        step = 1 << i
        up, upd = lift(e, step), lift(ed, step)
        e, ed = e + fade * up, ed + fade * (upd + float(step * length) * up)
    return lift(e, 1), lift(ed, 1), e[0:1], ed[0:1]


def farthest_first(n):
    return sorted(range(1, n), key=lambda r: -min(r, n - r))


def total_over(rows):
    return jnp.sum(rows, axis=0, keepdims=True)


def kernel(
    ctx_n, chan_n,
    x_hbm, g_hbm, res_hbm, rate_hbm, y_ref, small_ref,
    rows_x, rows_g, rows_y, rows_f, table_ref, corr_ref, par, out_stats, stats,
    x_ref, g_ref, res_ref, rate_ref, load_sem,
    par_send, par_recv, stats_send, stats_recv,
):
    ctx, chan = lax.axis_index("ctx"), lax.axis_index("chan")
    channels, span = x_ref.shape
    modes = res_ref.shape[1]
    chunks = span // LANES

    loads = [
        pltpu.make_async_copy(source, target, load_sem.at[i])
        for i, (source, target) in enumerate(
            [(res_hbm, res_ref), (rate_hbm, rate_ref), (x_hbm, x_ref), (g_hbm, g_ref)]
        )
    ]
    loads[0].start()
    loads[1].start()
    barrier = pltpu.get_barrier_semaphore()
    for r in farthest_first(chan_n):
        pl.semaphore_signal(
            barrier, inc=1, device_id={"chan": lax.rem(chan + r, chan_n)}, device_id_type=MESH
        )
    for r in range(1, ctx_n):
        pl.semaphore_signal(
            barrier, inc=1, device_id={"ctx": lax.rem(ctx + r, ctx_n)}, device_id_type=MESH
        )
    loads[2].start()
    loads[3].start()

    def exchange(buf, axis, me, n, send, recv):
        copies = []
        for r in farthest_first(n):
            copies.append(
                pltpu.make_async_remote_copy(
                    src_ref=buf.at[me],
                    dst_ref=buf.at[me],
                    send_sem=send,
                    recv_sem=recv,
                    device_id={axis: lax.rem(me + r, n)},
                    device_id_type=MESH,
                )
            )
        for copy in copies:
            copy.start()

    loads[0].wait()
    loads[1].wait()
    repeats = LANES // modes
    par[chan, 0:1, :] = jnp.concatenate([res_ref[...]] * repeats, axis=1)
    par[chan, 1:2, :] = jnp.concatenate([rate_ref[...]] * repeats, axis=1)

    pl.semaphore_wait(barrier, chan_n - 1 + ctx_n - 1)
    exchange(par, "chan", chan, chan_n, par_send, par_recv)

    loads[2].wait()
    loads[3].wait()
    for n in range(chunks):
        rows_x[n * channels : (n + 1) * channels, :] = x_ref[:, n * LANES : (n + 1) * LANES].astype(F32)
        rows_g[n * channels : (n + 1) * channels, :] = g_ref[:, n * LANES : (n + 1) * LANES].astype(F32)
    xs = [rows_x[pl.ds(c, chunks, stride=channels), :].astype(BF16) for c in range(channels)]
    gs = [rows_g[pl.ds(c, chunks, stride=channels), :].astype(BF16) for c in range(channels)]
    down, across = iota((LANES, LANES), 0), iota((LANES, LANES), 1)
    lane8 = iota((8, LANES), 1)
    for c in range(channels):
        gram = lax.dot_general(xs[c], gs[c], (((0,), (0,)), ((), ())), preferred_element_type=F32)
        lags = gram[:8]
        for b in range(8, LANES, 8):
            moved = pltpu.roll(gram[b : b + 8], LANES - b, axis=1)
            lags += jnp.where(lane8 < LANES - b, moved, 0.0)
        corr_ref[c * 8 : (c + 1) * 8, :] = lags
    corr = corr_ref[pl.ds(0, channels, stride=8), :]
    for i in range(1, 8):
        moved = pltpu.roll(corr_ref[pl.ds(i, channels, stride=8), :], LANES - i, axis=1)
        corr += jnp.where(lane8 < LANES - i, moved, 0.0)

    others = par.at[pl.ds(0, chan_n - 1)]
    pltpu.make_async_copy(others, others, par_recv).wait()

    res8, rate8 = par[:, 0, :], par[:, 1, :]
    own = iota((chan_n, LANES), 1) // modes == iota((chan_n, LANES), 0)
    res = jnp.sum(jnp.where(own, res8, 0.0), axis=0, keepdims=True)
    rate = jnp.sum(jnp.where(own, rate8, 0.0), axis=0, keepdims=True)
    root = jnp.sqrt(rate)
    amp = res * root

    chunk_fades = scan_fades(rate, chunks, LANES)
    to_end = ((chunks - 1 - iota((chunks, LANES), 0)) * LANES).astype(F32)
    chunk_fade = jnp.exp(-rate * to_end)
    at = down.astype(F32)
    till = (LANES - down).astype(F32)
    decay_g, decay_x = jnp.exp(-rate * at), jnp.exp(-rate * till)

    def table(plain, weight):
        parts = split(plain), split(weight * plain)
        return jnp.concatenate(
            [jnp.concatenate([p[i] for p in parts], axis=1) for i in range(2)], axis=0
        )

    def twice(value):
        return jnp.concatenate([value, value], axis=1)

    corr_high, corr_low = split(corr)
    left_g = twice(jnp.concatenate(gs + [corr_high, corr_low], axis=0))
    left_x = twice(jnp.concatenate(xs, axis=0))
    raw_g = jnp.dot(left_g, table(decay_g, at), preferred_element_type=F32)
    raw_x = jnp.dot(left_x, table(decay_x, till), preferred_element_type=F32)
    lane_chan = iota((chunks, LANES), 1) // modes

    def by_channel(raw):
        plain = jnp.zeros((chunks, LANES), F32)
        weighted = plain
        for c in range(channels):
            part = raw[c * chunks : (c + 1) * chunks]
            plain = jnp.where(lane_chan == c, part[:, :LANES], plain)
            weighted = jnp.where(lane_chan == c, part[:, LANES:], weighted)
        return plain, weighted

    e, ed = by_channel(raw_g)
    x, xd = by_channel(raw_x)
    corr_rows = raw_g[channels * chunks :]
    corr_rows = corr_rows[:channels] + corr_rows[channels:]
    p_in = jnp.sum(jnp.where(own, corr_rows[:, :LANES], 0.0), axis=0, keepdims=True)
    pd_in = jnp.sum(jnp.where(own, corr_rows[:, LANES:], 0.0), axis=0, keepdims=True)

    h, hd, e1, ed1 = entering(e, ed, chunk_fades, LANES)
    x1 = total_over(chunk_fade * x)
    xd1 = total_over(chunk_fade * (xd + to_end * x))
    p1 = p_in + total_over(x * h)
    pd1 = pd_in + total_over(xd * h + x * hd)
    sums = [ed1, x1, xd1, p1, pd1]
    owner_row = iota((chan_n, LANES), 0)
    lane_group = iota((chan_n, LANES), 1) // modes
    for_owner = jnp.zeros((chan_n, LANES), F32)
    for q, value in enumerate(sums):
        moved = pltpu.roll(value, modes * q, axis=1) if q else value
        for_owner = jnp.where(lane_group == (owner_row + q) % chan_n, moved, for_owner)
    out_stats[:, 0, :] = jnp.broadcast_to(e1, (chan_n, LANES))
    out_stats[:, 1, :] = for_owner
    count = ctx_n * chan_n
    me = ctx * chan_n + chan

    @pl.loop(0, count - 1)
    def _(i):
        to = i + jnp.where(i >= me, 1, 0)
        to_chan = lax.rem(to, chan_n)
        pltpu.make_async_remote_copy(
            src_ref=out_stats.at[to_chan],
            dst_ref=stats.at[me],
            send_sem=stats_send,
            recv_sem=stats_recv,
            device_id={"ctx": lax.div(to, chan_n), "chan": to_chan},
            device_id_type=MESH,
        ).start()

    stats[me] = out_stats[chan]

    lag = jnp.where(across[:channels] == 0, 0, LANES - across[:channels]).astype(F32)
    amp8 = res8 * jnp.sqrt(rate8)
    samples = jnp.zeros((channels, LANES), F32)
    for k in range(modes):
        samples += amp8[:, k : k + 1] * jnp.exp(-rate8[:, k : k + 1] * lag)
    out_high, out_low = split((amp * decay_x).T)
    table_ref[:LANES, :] = jnp.concatenate([out_high, out_low], axis=1)
    table_ref[LANES:, :] = jnp.concatenate([out_high, jnp.zeros_like(out_low)], axis=1)

    def expand(states):
        outer = jnp.dot(
            jnp.concatenate(split(states), axis=1), table_ref[...], preferred_element_type=F32
        )
        return outer[:, :LANES] + outer[:, LANES:]

    local = expand(
        jnp.concatenate([jnp.where(lane_chan == c, h, 0.0) for c in range(channels)], axis=0)
    )
    for c in range(channels):
        spread = jnp.broadcast_to(samples[c : c + 1, :], (LANES, LANES))
        toeplitz = pltpu.roll(spread, 0, axis=1, stride=1, stride_axis=0)
        toeplitz = jnp.where(across <= down, toeplitz, 0.0)
        inner = jnp.dot(
            twice(gs[c]), jnp.concatenate(split(toeplitz), axis=0), preferred_element_type=F32
        )
        rows_y[pl.ds(c, chunks, stride=channels), :] = inner + local[c * chunks : (c + 1) * chunks]

    for n in range(chunks):
        rows_x[n * channels : (n + 1) * channels, :] = jnp.where(own, chunk_fade[n : n + 1], 0.0)
    ahead = iota((count, LANES), 0) - (me + 1)
    fade_in = jnp.exp(-rate * (jnp.maximum(ahead, 0) * span).astype(F32))
    rows_f[...] = jnp.where(ahead >= 0, fade_in, 0.0)
    span_fades = scan_fades(rate, count, span)

    everyone = stats.at[pl.ds(0, count - 1)]
    pltpu.make_async_copy(everyone, everyone, stats_send).wait()
    pltpu.make_async_copy(others, others, par_send).wait()
    pltpu.make_async_copy(everyone, everyone, stats_recv).wait()
    states, mine = stats[:, 0, :], stats[:, 1, :]
    enter = total_over(rows_f[...] * states)
    y = rows_y[...] + expand(rows_x[...] * enter)
    for n in range(chunks):
        y_ref[:, n * LANES : (n + 1) * LANES] = y[n * channels : (n + 1) * channels].astype(BF16)

    def shifted(value, q):
        return pltpu.roll(value, LANES - modes * q, axis=1)

    h, hd, _, _ = entering(states, mine, span_fades, span)
    x, xd = shifted(mine, 1), shifted(mine, 2)
    sums = total_over(mine)
    plain = shifted(sums, 3) + total_over(x * h)
    tilted = shifted(sums, 4) + total_over(xd * h + x * hd)
    final = jnp.concatenate([root * plain, amp * (0.5 * plain - rate * tilted)], axis=0)
    small_ref[...] = pltpu.roll(final, lax.rem(LANES - modes * chan, LANES), axis=1)


def solution(mesh):
    ctx_n, chan_n = mesh.shape["ctx"], mesh.shape["chan"]

    def on_device(signal, grad_out, residue, decay_rate):
        channels, span = signal.shape
        modes = residue.shape[1]
        count = channels * span // LANES
        pinned = [pltpu.with_memory_space_constraint(v, pltpu.HBM) for v in (signal, grad_out, residue, decay_rate)]
        vmem = pl.BlockSpec(memory_space=pltpu.VMEM)
        small = jax.ShapeDtypeStruct((2, LANES), F32)
        y, small = pl.pallas_call(
            functools.partial(kernel, ctx_n, chan_n),
            out_shape=(jax.ShapeDtypeStruct((channels, span), BF16), small),
            in_specs=[pl.BlockSpec(memory_space=pl.ANY)] * 4,
            out_specs=(vmem,) * 2,
            scratch_shapes=[
                pltpu.VMEM((count, LANES), F32),
                pltpu.VMEM((count, LANES), F32),
                pltpu.VMEM((count, LANES), F32),
                pltpu.VMEM((ctx_n * chan_n, LANES), F32),
                pltpu.VMEM((2 * LANES, 2 * LANES), BF16),
                pltpu.VMEM((channels * 8, LANES), F32),
                pltpu.VMEM((chan_n, 2, LANES), F32),
                pltpu.VMEM((chan_n, 2, LANES), F32),
                pltpu.VMEM((ctx_n * chan_n, 2, LANES), F32),
                pltpu.VMEM((channels, span), BF16),
                pltpu.VMEM((channels, span), BF16),
                pltpu.VMEM((1, modes), F32),
                pltpu.VMEM((1, modes), F32),
                pltpu.SemaphoreType.DMA((4,)),
                pltpu.SemaphoreType.DMA,
                pltpu.SemaphoreType.DMA,
                pltpu.SemaphoreType.DMA,
                pltpu.SemaphoreType.DMA,
            ],
            compiler_params=pltpu.CompilerParams(
                collective_id=0, has_side_effects=True, vmem_limit_bytes=32 * 2**20
            ),
        )(*pinned)
        return y, small[0:1, :modes], small[1:2, :modes]

    return jax.shard_map(
        on_device,
        mesh=mesh,
        in_specs=(
            P(None, ("ctx", "chan")),
            P(None, ("ctx", "chan")),
            P("chan", None),
            P("chan", None),
        ),
        out_specs=(P(None, ("ctx", "chan")), P("chan", None), P("chan", None)),
        check_vma=False,
    )
```

```python
import functools

import jax
import jax.numpy as jnp
from jax import lax
from jax.experimental import pallas as pl
from jax.experimental.pallas import tpu as pltpu
from jax.sharding import PartitionSpec as P

MESH = pl.DeviceIdType.MESH
LANES = 128
F32 = jnp.float32
BF16 = jnp.bfloat16


def split(value):
    high = value.astype(BF16)
    return high, (value - high.astype(F32)).astype(BF16)


def iota(shape, axis):
    return lax.broadcasted_iota(jnp.int32, shape, axis)


def lift(array, step):
    rows = array.shape[0]
    moved = pltpu.roll(array, rows - step, axis=0)
    return jnp.where(iota(array.shape, 0) < rows - step, moved, 0.0)


def scan_fades(rate, rows, length):
    return [jnp.exp(-rate * float(length << i)) for i in range((rows - 1).bit_length())]


def entering(e, ed, fades, length):
    for i, fade in enumerate(fades):
        step = 1 << i
        up, upd = lift(e, step), lift(ed, step)
        e, ed = e + fade * up, ed + fade * (upd + float(step * length) * up)
    return lift(e, 1), lift(ed, 1), e[0:1], ed[0:1]


def farthest_first(n):
    return sorted(range(1, n), key=lambda r: -min(r, n - r))


def total_over(rows):
    return jnp.sum(rows, axis=0, keepdims=True)


def kernel(
    ctx_n, chan_n,
    x_hbm, g_hbm, res_hbm, rate_hbm, y_ref, small_ref,
    rows_x, rows_g, rows_y, rows_f, table_ref, corr_ref, par, out_stats, stats,
    x_ref, g_ref, res_ref, rate_ref, load_sem,
    par_send, par_recv, stats_send, stats_recv,
):
    ctx, chan = lax.axis_index("ctx"), lax.axis_index("chan")
    channels, span = x_ref.shape
    modes = res_ref.shape[1]
    chunks = span // LANES

    loads = [
        pltpu.make_async_copy(source, target, load_sem.at[i])
        for i, (source, target) in enumerate(
            [(res_hbm, res_ref), (rate_hbm, rate_ref), (x_hbm, x_ref), (g_hbm, g_ref)]
        )
    ]
    barrier = pltpu.get_barrier_semaphore()
    for r in farthest_first(chan_n):
        pl.semaphore_signal(
            barrier, inc=1, device_id={"chan": lax.rem(chan + r, chan_n)}, device_id_type=MESH
        )
    loads[0].start()
    loads[1].start()
    for r in range(1, ctx_n):
        pl.semaphore_signal(
            barrier, inc=1, device_id={"ctx": lax.rem(ctx + r, ctx_n)}, device_id_type=MESH
        )
    loads[2].start()
    loads[3].start()

    def exchange(buf, axis, me, n, send, recv):
        copies = []
        for r in farthest_first(n):
            copies.append(
                pltpu.make_async_remote_copy(
                    src_ref=buf.at[me],
                    dst_ref=buf.at[me],
                    send_sem=send,
                    recv_sem=recv,
                    device_id={axis: lax.rem(me + r, n)},
                    device_id_type=MESH,
                )
            )
        for copy in copies:
            copy.start()

    loads[0].wait()
    loads[1].wait()
    repeats = LANES // modes
    par[chan, 0:1, :] = jnp.concatenate([res_ref[...]] * repeats, axis=1)
    par[chan, 1:2, :] = jnp.concatenate([rate_ref[...]] * repeats, axis=1)

    pl.semaphore_wait(barrier, chan_n - 1 + ctx_n - 1)
    exchange(par, "chan", chan, chan_n, par_send, par_recv)

    loads[2].wait()
    loads[3].wait()
    for n in range(chunks):
        rows_x[n * channels : (n + 1) * channels, :] = x_ref[:, n * LANES : (n + 1) * LANES].astype(F32)
        rows_g[n * channels : (n + 1) * channels, :] = g_ref[:, n * LANES : (n + 1) * LANES].astype(F32)
    xs = [rows_x[pl.ds(c, chunks, stride=channels), :].astype(BF16) for c in range(channels)]
    gs = [rows_g[pl.ds(c, chunks, stride=channels), :].astype(BF16) for c in range(channels)]
    down, across = iota((LANES, LANES), 0), iota((LANES, LANES), 1)
    lane8 = iota((8, LANES), 1)
    for c in range(channels):
        gram = lax.dot_general(xs[c], gs[c], (((0,), (0,)), ((), ())), preferred_element_type=F32)
        lags = gram[:8]
        for b in range(8, LANES, 8):
            moved = pltpu.roll(gram[b : b + 8], LANES - b, axis=1)
            lags += jnp.where(lane8 < LANES - b, moved, 0.0)
        corr_ref[c * 8 : (c + 1) * 8, :] = lags
    corr = corr_ref[pl.ds(0, channels, stride=8), :]
    for i in range(1, 8):
        moved = pltpu.roll(corr_ref[pl.ds(i, channels, stride=8), :], LANES - i, axis=1)
        corr += jnp.where(lane8 < LANES - i, moved, 0.0)

    others = par.at[pl.ds(0, chan_n - 1)]
    pltpu.make_async_copy(others, others, par_recv).wait()

    res8, rate8 = par[:, 0, :], par[:, 1, :]
    own = iota((chan_n, LANES), 1) // modes == iota((chan_n, LANES), 0)
    res = jnp.sum(jnp.where(own, res8, 0.0), axis=0, keepdims=True)
    rate = jnp.sum(jnp.where(own, rate8, 0.0), axis=0, keepdims=True)
    root = jnp.sqrt(rate)
    amp = res * root

    chunk_fades = scan_fades(rate, chunks, LANES)
    to_end = ((chunks - 1 - iota((chunks, LANES), 0)) * LANES).astype(F32)
    chunk_fade = jnp.exp(-rate * to_end)
    at = down.astype(F32)
    till = (LANES - down).astype(F32)
    decay_g, decay_x = jnp.exp(-rate * at), jnp.exp(-rate * till)

    def table(plain, weight):
        parts = split(plain), split(weight * plain)
        return jnp.concatenate(
            [jnp.concatenate([p[i] for p in parts], axis=1) for i in range(2)], axis=0
        )

    def twice(value):
        return jnp.concatenate([value, value], axis=1)

    corr_high, corr_low = split(corr)
    left_g = twice(jnp.concatenate(gs + [corr_high, corr_low], axis=0))
    left_x = twice(jnp.concatenate(xs, axis=0))
    raw_g = jnp.dot(left_g, table(decay_g, at), preferred_element_type=F32)
    raw_x = jnp.dot(left_x, table(decay_x, till), preferred_element_type=F32)
    lane_chan = iota((chunks, LANES), 1) // modes

    def by_channel(raw):
        plain = jnp.zeros((chunks, LANES), F32)
        weighted = plain
        for c in range(channels):
            part = raw[c * chunks : (c + 1) * chunks]
            plain = jnp.where(lane_chan == c, part[:, :LANES], plain)
            weighted = jnp.where(lane_chan == c, part[:, LANES:], weighted)
        return plain, weighted

    e, ed = by_channel(raw_g)
    x, xd = by_channel(raw_x)
    corr_rows = raw_g[channels * chunks :]
    corr_rows = corr_rows[:channels] + corr_rows[channels:]
    p_in = jnp.sum(jnp.where(own, corr_rows[:, :LANES], 0.0), axis=0, keepdims=True)
    pd_in = jnp.sum(jnp.where(own, corr_rows[:, LANES:], 0.0), axis=0, keepdims=True)

    h, hd, e1, ed1 = entering(e, ed, chunk_fades, LANES)
    x1 = total_over(chunk_fade * x)
    xd1 = total_over(chunk_fade * (xd + to_end * x))
    p1 = p_in + total_over(x * h)
    pd1 = pd_in + total_over(xd * h + x * hd)
    sums = [ed1, x1, xd1, p1, pd1]
    owner_row = iota((chan_n, LANES), 0)
    lane_group = iota((chan_n, LANES), 1) // modes
    for_owner = jnp.zeros((chan_n, LANES), F32)
    for q, value in enumerate(sums):
        moved = pltpu.roll(value, modes * q, axis=1) if q else value
        for_owner = jnp.where(lane_group == (owner_row + q) % chan_n, moved, for_owner)
    out_stats[:, 0, :] = jnp.broadcast_to(e1, (chan_n, LANES))
    out_stats[:, 1, :] = for_owner
    count = ctx_n * chan_n
    me = ctx * chan_n + chan

    @pl.loop(0, count - 1)
    def _(i):
        to = i + jnp.where(i >= me, 1, 0)
        to_chan = lax.rem(to, chan_n)
        pltpu.make_async_remote_copy(
            src_ref=out_stats.at[to_chan],
            dst_ref=stats.at[me],
            send_sem=stats_send,
            recv_sem=stats_recv,
            device_id={"ctx": lax.div(to, chan_n), "chan": to_chan},
            device_id_type=MESH,
        ).start()

    stats[me] = out_stats[chan]

    lag = jnp.where(across[:channels] == 0, 0, LANES - across[:channels]).astype(F32)
    amp8 = res8 * jnp.sqrt(rate8)
    samples = jnp.zeros((channels, LANES), F32)
    for k in range(modes):
        samples += amp8[:, k : k + 1] * jnp.exp(-rate8[:, k : k + 1] * lag)
    out_high, out_low = split((amp * decay_x).T)
    table_ref[:LANES, :] = jnp.concatenate([out_high, out_low], axis=1)
    table_ref[LANES:, :] = jnp.concatenate([out_high, jnp.zeros_like(out_low)], axis=1)

    def expand(states):
        outer = jnp.dot(
            jnp.concatenate(split(states), axis=1), table_ref[...], preferred_element_type=F32
        )
        return outer[:, :LANES] + outer[:, LANES:]

    local = expand(
        jnp.concatenate([jnp.where(lane_chan == c, h, 0.0) for c in range(channels)], axis=0)
    )
    for c in range(channels):
        spread = jnp.broadcast_to(samples[c : c + 1, :], (LANES, LANES))
        toeplitz = pltpu.roll(spread, 0, axis=1, stride=1, stride_axis=0)
        toeplitz = jnp.where(across <= down, toeplitz, 0.0)
        inner = jnp.dot(
            twice(gs[c]), jnp.concatenate(split(toeplitz), axis=0), preferred_element_type=F32
        )
        rows_y[pl.ds(c, chunks, stride=channels), :] = inner + local[c * chunks : (c + 1) * chunks]

    for n in range(chunks):
        rows_x[n * channels : (n + 1) * channels, :] = jnp.where(own, chunk_fade[n : n + 1], 0.0)
    ahead = iota((count, LANES), 0) - (me + 1)
    fade_in = jnp.exp(-rate * (jnp.maximum(ahead, 0) * span).astype(F32))
    rows_f[...] = jnp.where(ahead >= 0, fade_in, 0.0)
    span_fades = scan_fades(rate, count, span)

    everyone = stats.at[pl.ds(0, count - 1)]
    pltpu.make_async_copy(everyone, everyone, stats_send).wait()
    pltpu.make_async_copy(others, others, par_send).wait()
    pltpu.make_async_copy(everyone, everyone, stats_recv).wait()
    states, mine = stats[:, 0, :], stats[:, 1, :]
    enter = total_over(rows_f[...] * states)
    y = rows_y[...] + expand(rows_x[...] * enter)
    for n in range(chunks):
        y_ref[:, n * LANES : (n + 1) * LANES] = y[n * channels : (n + 1) * channels].astype(BF16)

    def shifted(value, q):
        return pltpu.roll(value, LANES - modes * q, axis=1)

    h, hd, _, _ = entering(states, mine, span_fades, span)
    x, xd = shifted(mine, 1), shifted(mine, 2)
    sums = total_over(mine)
    plain = shifted(sums, 3) + total_over(x * h)
    tilted = shifted(sums, 4) + total_over(xd * h + x * hd)
    final = jnp.concatenate([root * plain, amp * (0.5 * plain - rate * tilted)], axis=0)
    small_ref[...] = pltpu.roll(final, lax.rem(LANES - modes * chan, LANES), axis=1)


def solution(mesh):
    ctx_n, chan_n = mesh.shape["ctx"], mesh.shape["chan"]

    def on_device(signal, grad_out, residue, decay_rate):
        channels, span = signal.shape
        modes = residue.shape[1]
        count = channels * span // LANES
        pinned = [pltpu.with_memory_space_constraint(v, pltpu.HBM) for v in (signal, grad_out, residue, decay_rate)]
        vmem = pl.BlockSpec(memory_space=pltpu.VMEM)
        small = jax.ShapeDtypeStruct((2, LANES), F32)
        y, small = pl.pallas_call(
            functools.partial(kernel, ctx_n, chan_n),
            out_shape=(jax.ShapeDtypeStruct((channels, span), BF16), small),
            in_specs=[pl.BlockSpec(memory_space=pl.ANY)] * 4,
            out_specs=(vmem,) * 2,
            scratch_shapes=[
                pltpu.VMEM((count, LANES), F32),
                pltpu.VMEM((count, LANES), F32),
                pltpu.VMEM((count, LANES), F32),
                pltpu.VMEM((ctx_n * chan_n, LANES), F32),
                pltpu.VMEM((2 * LANES, 2 * LANES), BF16),
                pltpu.VMEM((channels * 8, LANES), F32),
                pltpu.VMEM((chan_n, 2, LANES), F32),
                pltpu.VMEM((chan_n, 2, LANES), F32),
                pltpu.VMEM((ctx_n * chan_n, 2, LANES), F32),
                pltpu.VMEM((channels, span), BF16),
                pltpu.VMEM((channels, span), BF16),
                pltpu.VMEM((1, modes), F32),
                pltpu.VMEM((1, modes), F32),
                pltpu.SemaphoreType.DMA((4,)),
                pltpu.SemaphoreType.DMA,
                pltpu.SemaphoreType.DMA,
                pltpu.SemaphoreType.DMA,
                pltpu.SemaphoreType.DMA,
            ],
            compiler_params=pltpu.CompilerParams(
                collective_id=0, has_side_effects=True, vmem_limit_bytes=32 * 2**20
            ),
        )(*pinned)
        return y, small[0:1, :modes], small[1:2, :modes]

    return jax.shard_map(
        on_device,
        mesh=mesh,
        in_specs=(
            P(None, ("ctx", "chan")),
            P(None, ("ctx", "chan")),
            P("chan", None),
            P("chan", None),
        ),
        out_specs=(P(None, ("ctx", "chan")), P("chan", None), P("chan", None)),
        check_vma=False,
    )
```

```python
import functools

import jax
import jax.numpy as jnp
from jax import lax
from jax.experimental import pallas as pl
from jax.experimental.pallas import tpu as pltpu
from jax.sharding import PartitionSpec as P

MESH = pl.DeviceIdType.MESH
LANES = 128
F32 = jnp.float32
BF16 = jnp.bfloat16


def split(value):
    high = value.astype(BF16)
    return high, (value - high.astype(F32)).astype(BF16)


def iota(shape, axis):
    return lax.broadcasted_iota(jnp.int32, shape, axis)


def lift(array, step):
    rows = array.shape[0]
    moved = pltpu.roll(array, rows - step, axis=0)
    return jnp.where(iota(array.shape, 0) < rows - step, moved, 0.0)


def scan_fades(rate, rows, length):
    return [jnp.exp(-rate * float(length << i)) for i in range((rows - 1).bit_length())]


def entering(e, ed, fades, length):
    for i, fade in enumerate(fades):
        step = 1 << i
        up, upd = lift(e, step), lift(ed, step)
        e, ed = e + fade * up, ed + fade * (upd + float(step * length) * up)
    return lift(e, 1), lift(ed, 1), e[0:1], ed[0:1]


def farthest_first(n):
    return sorted(range(1, n), key=lambda r: -min(r, n - r))


def total_over(rows):
    return jnp.sum(rows, axis=0, keepdims=True)


def kernel(
    ctx_n, chan_n,
    x_hbm, g_hbm, res_hbm, rate_hbm, y_ref, small_ref,
    rows_x, rows_g, rows_y, rows_f, corr_ref, par, out_stats, stats,
    x_ref, g_ref, res_ref, rate_ref, load_sem,
    par_send, par_recv, stats_send, stats_recv,
):
    ctx, chan = lax.axis_index("ctx"), lax.axis_index("chan")
    channels, span = x_ref.shape
    modes = res_ref.shape[1]
    chunks = span // LANES

    loads = [
        pltpu.make_async_copy(source, target, load_sem.at[i])
        for i, (source, target) in enumerate(
            [(res_hbm, res_ref), (rate_hbm, rate_ref), (x_hbm, x_ref), (g_hbm, g_ref)]
        )
    ]
    loads[0].start()
    loads[1].start()
    barrier = pltpu.get_barrier_semaphore()
    for r in farthest_first(chan_n):
        pl.semaphore_signal(
            barrier, inc=1, device_id={"chan": lax.rem(chan + r, chan_n)}, device_id_type=MESH
        )
    for r in range(1, ctx_n):
        pl.semaphore_signal(
            barrier, inc=1, device_id={"ctx": lax.rem(ctx + r, ctx_n)}, device_id_type=MESH
        )
    loads[2].start()
    loads[3].start()

    def exchange(buf, axis, me, n, send, recv):
        copies = []
        for r in farthest_first(n):
            copies.append(
                pltpu.make_async_remote_copy(
                    src_ref=buf.at[me],
                    dst_ref=buf.at[me],
                    send_sem=send,
                    recv_sem=recv,
                    device_id={axis: lax.rem(me + r, n)},
                    device_id_type=MESH,
                )
            )
        for copy in copies:
            copy.start()

    loads[0].wait()
    loads[1].wait()
    repeats = LANES // modes
    par[chan, 0:1, :] = jnp.concatenate([res_ref[...]] * repeats, axis=1)
    par[chan, 1:2, :] = jnp.concatenate([rate_ref[...]] * repeats, axis=1)

    pl.semaphore_wait(barrier, chan_n - 1 + ctx_n - 1)
    exchange(par, "chan", chan, chan_n, par_send, par_recv)

    loads[2].wait()
    loads[3].wait()
    for n in range(chunks):
        rows_x[n * channels : (n + 1) * channels, :] = x_ref[:, n * LANES : (n + 1) * LANES].astype(F32)
        rows_g[n * channels : (n + 1) * channels, :] = g_ref[:, n * LANES : (n + 1) * LANES].astype(F32)
    xs = [rows_x[pl.ds(c, chunks, stride=channels), :].astype(BF16) for c in range(channels)]
    gs = [rows_g[pl.ds(c, chunks, stride=channels), :].astype(BF16) for c in range(channels)]
    down, across = iota((LANES, LANES), 0), iota((LANES, LANES), 1)
    lane8 = iota((8, LANES), 1)
    for c in range(channels):
        gram = lax.dot_general(xs[c], gs[c], (((0,), (0,)), ((), ())), preferred_element_type=F32)
        lags = gram[:8]
        for b in range(8, LANES, 8):
            moved = pltpu.roll(gram[b : b + 8], LANES - b, axis=1)
            lags += jnp.where(lane8 < LANES - b, moved, 0.0)
        corr_ref[c * 8 : (c + 1) * 8, :] = lags
    corr = corr_ref[pl.ds(0, channels, stride=8), :]
    for i in range(1, 8):
        moved = pltpu.roll(corr_ref[pl.ds(i, channels, stride=8), :], LANES - i, axis=1)
        corr += jnp.where(lane8 < LANES - i, moved, 0.0)

    others = par.at[pl.ds(0, chan_n - 1)]
    pltpu.make_async_copy(others, others, par_recv).wait()

    res8, rate8 = par[:, 0, :], par[:, 1, :]
    own = iota((chan_n, LANES), 1) // modes == iota((chan_n, LANES), 0)
    res = jnp.sum(jnp.where(own, res8, 0.0), axis=0, keepdims=True)
    rate = jnp.sum(jnp.where(own, rate8, 0.0), axis=0, keepdims=True)
    root = jnp.sqrt(rate)
    amp = res * root

    chunk_fades = scan_fades(rate, chunks, LANES)
    to_end = ((chunks - 1 - iota((chunks, LANES), 0)) * LANES).astype(F32)
    chunk_fade = jnp.exp(-rate * to_end)
    at = down.astype(F32)
    till = (LANES - down).astype(F32)
    decay_g, decay_x = jnp.exp(-rate * at), jnp.exp(-rate * till)

    def table(plain, weight):
        parts = split(plain), split(weight * plain)
        return jnp.concatenate(
            [jnp.concatenate([p[i] for p in parts], axis=1) for i in range(2)], axis=0
        )

    def twice(value):
        return jnp.concatenate([value, value], axis=1)

    corr_high, corr_low = split(corr)
    left_g = twice(jnp.concatenate(gs + [corr_high, corr_low], axis=0))
    left_x = twice(jnp.concatenate(xs, axis=0))
    raw_g = jnp.dot(left_g, table(decay_g, at), preferred_element_type=F32)
    raw_x = jnp.dot(left_x, table(decay_x, till), preferred_element_type=F32)
    lane_chan = iota((chunks, LANES), 1) // modes

    def by_channel(raw):
        plain = jnp.zeros((chunks, LANES), F32)
        weighted = plain
        for c in range(channels):
            part = raw[c * chunks : (c + 1) * chunks]
            plain = jnp.where(lane_chan == c, part[:, :LANES], plain)
            weighted = jnp.where(lane_chan == c, part[:, LANES:], weighted)
        return plain, weighted

    e, ed = by_channel(raw_g)
    x, xd = by_channel(raw_x)
    corr_rows = raw_g[channels * chunks :]
    corr_rows = corr_rows[:channels] + corr_rows[channels:]
    p_in = jnp.sum(jnp.where(own, corr_rows[:, :LANES], 0.0), axis=0, keepdims=True)
    pd_in = jnp.sum(jnp.where(own, corr_rows[:, LANES:], 0.0), axis=0, keepdims=True)

    h, hd, e1, ed1 = entering(e, ed, chunk_fades, LANES)
    x1 = total_over(chunk_fade * x)
    xd1 = total_over(chunk_fade * (xd + to_end * x))
    p1 = p_in + total_over(x * h)
    pd1 = pd_in + total_over(xd * h + x * hd)
    sums = [ed1, x1, xd1, p1, pd1]
    owner_row = iota((chan_n, LANES), 0)
    lane_group = iota((chan_n, LANES), 1) // modes
    for_owner = jnp.zeros((chan_n, LANES), F32)
    for q, value in enumerate(sums):
        moved = pltpu.roll(value, modes * q, axis=1) if q else value
        for_owner = jnp.where(lane_group == (owner_row + q) % chan_n, moved, for_owner)
    out_stats[:, 0, :] = jnp.broadcast_to(e1, (chan_n, LANES))
    out_stats[:, 1, :] = for_owner
    count = ctx_n * chan_n
    me = ctx * chan_n + chan

    def send(line, to_chan):
        pltpu.make_async_remote_copy(
            src_ref=out_stats.at[to_chan],
            dst_ref=stats.at[me],
            send_sem=stats_send,
            recv_sem=stats_recv,
            device_id={"ctx": line, "chan": to_chan},
            device_id_type=MESH,
        ).start()

    @pl.loop(0, ctx_n - 1)
    def _(i):
        line = i + jnp.where(i >= ctx, 1, 0)
        for c in range(chan_n):
            send(line, c)

    for r in farthest_first(chan_n):
        send(ctx, lax.rem(chan + r, chan_n))

    stats[me] = out_stats[chan]

    lag = jnp.where(across[:channels] == 0, 0, LANES - across[:channels]).astype(F32)
    amp8 = res8 * jnp.sqrt(rate8)
    samples = jnp.zeros((channels, LANES), F32)
    for k in range(modes):
        samples += amp8[:, k : k + 1] * jnp.exp(-rate8[:, k : k + 1] * lag)
    out_high, out_low = split(amp * decay_x)
    out_table = jnp.concatenate(
        [twice(out_high), jnp.concatenate([out_low, jnp.zeros_like(out_low)], axis=1)], axis=0
    )

    def expand(states):
        outer = lax.dot_general(
            jnp.concatenate(split(states), axis=1),
            out_table,
            (((1,), (1,)), ((), ())),
            preferred_element_type=F32,
        )
        return outer[:, :LANES] + outer[:, LANES:]

    local = expand(
        jnp.concatenate([jnp.where(lane_chan == c, h, 0.0) for c in range(channels)], axis=0)
    )
    for c in range(channels):
        spread = jnp.broadcast_to(samples[c : c + 1, :], (LANES, LANES))
        toeplitz = pltpu.roll(spread, 0, axis=1, stride=1, stride_axis=0)
        toeplitz = jnp.where(across <= down, toeplitz, 0.0)
        inner = jnp.dot(
            twice(gs[c]), jnp.concatenate(split(toeplitz), axis=0), preferred_element_type=F32
        )
        rows_y[pl.ds(c, chunks, stride=channels), :] = inner + local[c * chunks : (c + 1) * chunks]

    for n in range(chunks):
        rows_x[n * channels : (n + 1) * channels, :] = jnp.where(own, chunk_fade[n : n + 1], 0.0)
    ahead = iota((count, LANES), 0) - (me + 1)
    fade_in = jnp.exp(-rate * (jnp.maximum(ahead, 0) * span).astype(F32))
    rows_f[...] = jnp.where(ahead >= 0, fade_in, 0.0)
    span_fades = scan_fades(rate, count, span)

    everyone = stats.at[pl.ds(0, count - 1)]
    pltpu.make_async_copy(everyone, everyone, stats_send).wait()
    pltpu.make_async_copy(others, others, par_send).wait()
    pltpu.make_async_copy(everyone, everyone, stats_recv).wait()
    states, mine = stats[:, 0, :], stats[:, 1, :]
    enter = total_over(rows_f[...] * states)
    y = rows_y[...] + expand(rows_x[...] * enter)
    for n in range(chunks):
        y_ref[:, n * LANES : (n + 1) * LANES] = y[n * channels : (n + 1) * channels].astype(BF16)

    def shifted(value, q):
        return pltpu.roll(value, LANES - modes * q, axis=1)

    h, hd, _, _ = entering(states, mine, span_fades, span)
    x, xd = shifted(mine, 1), shifted(mine, 2)
    sums = total_over(mine)
    plain = shifted(sums, 3) + total_over(x * h)
    tilted = shifted(sums, 4) + total_over(xd * h + x * hd)
    final = jnp.concatenate([root * plain, amp * (0.5 * plain - rate * tilted)], axis=0)
    small_ref[...] = pltpu.roll(final, lax.rem(LANES - modes * chan, LANES), axis=1)


def solution(mesh):
    ctx_n, chan_n = mesh.shape["ctx"], mesh.shape["chan"]

    def on_device(signal, grad_out, residue, decay_rate):
        channels, span = signal.shape
        modes = residue.shape[1]
        count = channels * span // LANES
        pinned = [pltpu.with_memory_space_constraint(v, pltpu.HBM) for v in (signal, grad_out, residue, decay_rate)]
        vmem = pl.BlockSpec(memory_space=pltpu.VMEM)
        small = jax.ShapeDtypeStruct((2, LANES), F32)
        y, small = pl.pallas_call(
            functools.partial(kernel, ctx_n, chan_n),
            out_shape=(jax.ShapeDtypeStruct((channels, span), BF16), small),
            in_specs=[pl.BlockSpec(memory_space=pl.ANY)] * 4,
            out_specs=(vmem,) * 2,
            scratch_shapes=[
                pltpu.VMEM((count, LANES), F32),
                pltpu.VMEM((count, LANES), F32),
                pltpu.VMEM((count, LANES), F32),
                pltpu.VMEM((ctx_n * chan_n, LANES), F32),
                pltpu.VMEM((channels * 8, LANES), F32),
                pltpu.VMEM((chan_n, 2, LANES), F32),
                pltpu.VMEM((chan_n, 2, LANES), F32),
                pltpu.VMEM((ctx_n * chan_n, 2, LANES), F32),
                pltpu.VMEM((channels, span), BF16),
                pltpu.VMEM((channels, span), BF16),
                pltpu.VMEM((1, modes), F32),
                pltpu.VMEM((1, modes), F32),
                pltpu.SemaphoreType.DMA((4,)),
                pltpu.SemaphoreType.DMA,
                pltpu.SemaphoreType.DMA,
                pltpu.SemaphoreType.DMA,
                pltpu.SemaphoreType.DMA,
            ],
            compiler_params=pltpu.CompilerParams(
                collective_id=0, has_side_effects=True, vmem_limit_bytes=32 * 2**20
            ),
        )(*pinned)
        return y, small[0:1, :modes], small[1:2, :modes]

    return jax.shard_map(
        on_device,
        mesh=mesh,
        in_specs=(
            P(None, ("ctx", "chan")),
            P(None, ("ctx", "chan")),
            P("chan", None),
            P("chan", None),
        ),
        out_specs=(P(None, ("ctx", "chan")), P("chan", None), P("chan", None)),
        check_vma=False,
    )
```
